128 devices in a mesh: gx: 16 (over x, y), gy: 8 (over z, core).
Axes of the slice: x: 4, y: 4, z: 4, core: 2. Of those that a mesh axis runs over, the one named last changes fastest.
Arguments:
- adj_head: float32 [256, 256, 256], P('gx', 'gy'), may hold values from -6 to 6
- adj_species: float32 [6, 256, 256, 256], P(None, 'gx', 'gy'), may hold values from -6 to 6
- cond: float32 [256, 256, 256], P('gx', 'gy'), may hold values from 0.1 to 1
- capacity: float32 [256, 256, 256], P('gx', 'gy'), may hold values from 0.5 to 2
- rate: float32 [256, 256, 256], P('gx', 'gy'), may hold values from 0.1 to 1
- diffusion: float32 [6], replicated, may hold values from 0.05 to 0.3
- coupling: float32 [6], replicated, may hold values from -3 to 3
- react: float32 [4, 6, 6], replicated, may hold values from -6 to 6
- material: int32 [256, 256, 256], P('gx', 'gy'), may hold values from 0 to 3
- drain_mask: int32 [256, 256, 256], P('gx', 'gy'), may hold values 0 or 1
- block_pipe: int32 [256, 256, 2], P('gx', 'gy'), may hold values from 0 to 255
- pipe_obs: float32 [7, 16, 256], P(None, 'gx', 'gy'), may hold values from -6 to 6
Outputs:
- head_out: float32 [256, 256, 256], P('gx', 'gy')
- species_out: float32 [6, 256, 256, 256], P(None, 'gx', 'gy')
The draws below stay inside these ranges and needn't reach their ends.
All inputs are finite; a program needn't handle non-finite values. No bound on the sum of `drain_mask` on one device may be relied on, other than what follows from the above.
Results may differ from the reference program's by a relative error of at most 0.0003.
Values sent between devices are 32-bit elements; how exact they have to be, the bound alone decides.
No kernel may reach another device: no remote copies, remote signals or barrier semaphores. Data moves between devices by JAX's collectives and lax.ppermute only.
A program may use at most 128 MiB of HBM per device.

```python
import math
import jax
import jax.numpy as jnp
import numpy as np
from jax import lax

CX = 16
NZ = 256
NSPEC = 6
NMAT = 4
ITERS = 3
NZB = 2
PIPES = 256
NX = 256
NY = 256
N_GX = 16


def place_ends(drawn, rng, low, high):
    index_at = [jax.random.randint(jax.random.fold_in(rng, axis), (), 0, length) for axis, length in enumerate(drawn.shape)]
    main_axis = drawn.shape.index(max(drawn.shape))
    beside = index_at[:main_axis] + [(index_at[main_axis] + 1) % drawn.shape[main_axis]] + index_at[main_axis + 1:]
    return drawn.at[tuple(index_at)].set(low).at[tuple(beside)].set(high)


def steps_of(own_key, shape, shards, least, top_value):
    def one(position, blocks):
        draws = jax.random.uniform(jax.random.fold_in(jax.random.fold_in(own_key, 6), position), (blocks,), jnp.float32, least / len(shards), top_value / len(shards))
        return jnp.repeat(jnp.exp(draws), shape[position] // blocks).reshape((-1,) + (1,) * (len(shape) - position - 1))

    factor_of = one(*shards[0])
    for cut in shards[1:]:
        factor_of = factor_of * one(*cut)
    return factor_of


def rank_table(amount, lean):
    loads = [(1 << 20) // math.isqrt(rank ** lean) + 1 for rank in range(1, amount + 1)]
    scale = 1 + sum(loads) // (1 << 30)
    return np.cumsum(np.array([max(1, weight // scale) for weight in loads]))


def ranked_ids(key, shape, number_of, slope):
    table = rank_table(number_of, slope)
    pick = jax.random.randint(jax.random.fold_in(key, 1), shape, 0, int(table[number_of - 1]))
    grade = jnp.searchsorted(jnp.asarray(table, jnp.int32), pick, side="right")
    return jax.random.permutation(jax.random.fold_in(key, 2), number_of)[grade].astype(jnp.int32)


def normal_values(rng, dims, deviation, most, shards=(), kind=jnp.bfloat16):
    factor_of = steps_of(rng, dims, shards, -0.22, 0.18) if shards else 1.0
    array = jax.random.normal(rng, dims, jnp.float32) * deviation * factor_of
    return jnp.minimum(jnp.maximum(array, -most), most).astype(kind)


def setup_inputs(seed: int = 0) -> dict:
    splits = jax.random.split(jax.random.key(seed), 13)
    adj_head = normal_values(splits[0], (NX, NY, NZ), 1.0, 6.0, ((0, 16), (1, 8)), jnp.float32)
    adj_species = normal_values(splits[1], (NSPEC, NX, NY, NZ), 1.0, 6.0, ((1, 16), (2, 8)), jnp.float32)
    cond = jnp.clip(jnp.exp(math.log(1.0) - 2.3025851 * jax.random.uniform(splits[2], (NX, NY, NZ), jnp.float32) ** steps_of(splits[2], (NX, NY, NZ), ((0, 16), (1, 8)), -0.2, 0.2)), 0.1, 1.0)
    capacity = jnp.clip(jnp.exp(math.log(2.0) - 1.3862944 * jax.random.uniform(splits[3], (NX, NY, NZ), jnp.float32) ** steps_of(splits[3], (NX, NY, NZ), ((0, 16), (1, 8)), -0.2, 0.2)), 0.5, 2.0)
    rate = jnp.clip(jnp.exp(math.log(1.0) - 2.3025851 * jax.random.uniform(splits[4], (NX, NY, NZ), jnp.float32) ** steps_of(splits[4], (NX, NY, NZ), ((0, 16), (1, 8)), -0.2, 0.2)), 0.1, 1.0)
    diffusion = jnp.clip(jnp.exp(jax.random.uniform(splits[5], (NSPEC,), jnp.float32, math.log(0.05), math.log(0.3))), 0.05, 0.3)
    coupling = normal_values(splits[6], (NSPEC,), 1.0, 3.0, (), jnp.float32)
    react = normal_values(splits[7], (NMAT, NSPEC, NSPEC), 1 ** -0.5, 6.0, (), jnp.float32)
    material = place_ends(jax.random.randint(splits[8], (NX, NY, NZ), 0, NMAT), jax.random.fold_in(splits[8], 1), 0, NMAT - 1).astype(jnp.int32)
    drain_mask = place_ends((jax.random.randint(splits[9], (NX, NY, NZ), 0, 2) < 1).astype(jnp.int32), jax.random.fold_in(splits[9], 1), 0, 1)
    block_pipe = place_ends(ranked_ids(splits[10], (NX, NY, NZB), PIPES, 2), jax.random.fold_in(splits[10], 3), 0, PIPES - 1).astype(jnp.int32)
    pipe_obs = normal_values(splits[11], (NSPEC + 1, N_GX, PIPES), 1.0, 6.0, ((1, 16), (2, 8)), jnp.float32)
    return {"adj_head": adj_head, "adj_species": adj_species, "cond": cond, "capacity": capacity, "rate": rate, "diffusion": diffusion, "coupling": coupling, "react": react, "material": material, "drain_mask": drain_mask, "block_pipe": block_pipe, "pipe_obs": pipe_obs}


time_step = 0.08
drain_gain = 0.5

def neighbours(field):
    lead = [(0, 0)] * (field.ndim - 3)
    padded = jnp.pad(field, lead + [(1, 1)] * 3)
    return [padded[..., 2:, 1:-1, 1:-1], padded[..., :-2, 1:-1, 1:-1], padded[..., 1:-1, 2:, 1:-1], padded[..., 1:-1, :-2, 1:-1], padded[..., 1:-1, 1:-1, 2:], padded[..., 1:-1, 1:-1, :-2]]

def flow_term(scaled, cond):
    total = jnp.zeros_like(scaled)
    for other, other_cond in zip(neighbours(scaled), neighbours(cond)):
        total = total + 0.5 * (cond + other_cond) * (other - scaled)
    return total

def spread_term(scaled):
    total = jnp.zeros_like(scaled)
    for other in neighbours(scaled):
        total = total + (other - scaled)
    return total

def reacted_term(adj_species, material, react):
    result = jnp.zeros_like(adj_species)
    for index in range(react.shape[0]):
        mixed = jnp.einsum('ts,txyz->sxyz', react[index], adj_species, precision=lax.Precision.HIGHEST)
        result = jnp.where(material[None] == index, mixed, result)
    return result

def reference(adj_head, adj_species, cond, capacity, rate, diffusion, coupling, react, material, drain_mask, block_pipe, pipe_obs):
    chans = NSPEC + 1
    mask_f = drain_mask.astype(jnp.float32)
    strips = (jnp.arange(NX, dtype=jnp.int32) // CX).astype(jnp.int32)
    pipe_ids = (strips[:, None, None] * PIPES + block_pipe).reshape(-1)
    total_pipes = N_GX * PIPES
    observed = pipe_obs.reshape(chans, total_pipes)
    block_counts = mask_f.reshape(NX, NY, NZB, 128).sum(-1).reshape(-1)
    pipe_count = jax.ops.segment_sum(block_counts, pipe_ids, total_pipes)
    for step_index in range(ITERS):
        channels = jnp.concatenate([(cond * adj_head)[None], adj_species], 0) * mask_f[None]
        blocks = channels.reshape(chans, NX, NY, NZB, 128).sum(-1).reshape(chans, -1)
        pipe_sum = jax.ops.segment_sum(blocks.T, pipe_ids, total_pipes).T
        answer = jnp.tanh(observed - pipe_sum / jnp.sqrt(pipe_count + 1.0)[None])
        back = answer[:, pipe_ids].reshape(chans, NX, NY, NZB, 1)
        back = jnp.broadcast_to(back, (chans, NX, NY, NZB, 128)).reshape(chans, NX, NY, NZ) * mask_f[None]
        scaled_head = time_step * adj_head / capacity
        scaled_species = time_step * diffusion[:, None, None, None] * adj_species
        flow = flow_term(scaled_head, cond)
        spread = spread_term(scaled_species)
        reacted = reacted_term(adj_species, material, react)
        source = lax.optimization_barrier(jnp.sum(coupling[:, None, None, None] * adj_species, axis=0))
        new_head = adj_head + flow + time_step * rate * source + drain_gain * back[0]
        new_species = adj_species + spread - time_step * rate[None] * reacted + drain_gain * back[1:]
        adj_head, adj_species = (new_head, new_species)
    return (adj_head, adj_species)
```

```python
import functools

import jax
import jax.numpy as jnp
from jax import lax
from jax.experimental import pallas as pl
from jax.experimental.pallas import tpu as pltpu
from jax.sharding import PartitionSpec as P

ITERS = 3
time_step = 0.08
drain_gain = 0.5

F32 = jnp.float32
BF16 = jnp.bfloat16
ANY = pl.BlockSpec(memory_space=pl.ANY)
VM = pl.BlockSpec(memory_space=pltpu.VMEM)
SM = pl.BlockSpec(memory_space=pltpu.SMEM)
TOP = 8
STEP = 4
RB = 16


def split3(x):
    hi = x.astype(BF16)
    rest = x - hi.astype(F32)
    mid = rest.astype(BF16)
    low = (rest - mid.astype(F32)).astype(BF16)
    return hi, mid, low


def block_onehot(bp, block, n_pipes):
    col = bp[:, :, block : block + 1]
    col = col.reshape(col.shape[0] * col.shape[1], 1)
    return (col == lax.broadcasted_iota(jnp.int32, (col.shape[0], n_pipes), 1)).astype(BF16)


def pipe_sums(block_sums, onehots, rows):
    total = None
    for sums, onehot in zip(block_sums, onehots):
        flat = jnp.transpose(sums)[:rows]
        for piece in split3(flat):
            part = jnp.dot(piece, onehot, preferred_element_type=F32)
            total = part if total is None else total + part
    return total


def first_kernel(
    rows, chans, h, sp, cond, cap, mask, bp, obs, sh, px1, px2, pa, pb, bsum
):
    step = pl.program_id(0)
    steps = pl.num_programs(0)
    even_x = lax.axis_index("gx") % 2 == 0
    gy = lax.axis_index("gy")
    even_y = gy % 2 == 0
    lane = lax.broadcasted_iota(jnp.int32, (rows, 128), 1)
    planes = h.shape[0]
    for i in range(planes):
        x = step * planes + i
        head = h[i]
        scaled = time_step * head / cap[i]
        sh[i] = scaled
        cd = cond[i]
        fields = [scaled] + [sp[c, i] for c in range(chans - 1)] + [cd]
        for c, field in enumerate(fields):
            lo, hi = field[0:1], field[rows - 1 : rows]
            pa[x, c : c + 1, :] = jnp.where(even_y, hi, lo)
            pb[x, c : c + 1, :] = jnp.where(even_y, lo, hi)

        if i == 0:

            @pl.when((step == 0) & even_x)
            def _():
                for c, field in enumerate(fields):
                    px2[c] = field

            @pl.when((step == 0) & jnp.logical_not(even_x))
            def _():
                for c, field in enumerate(fields):
                    px1[c] = field

        if i == planes - 1:

            @pl.when((step == steps - 1) & even_x)
            def _():
                for c, field in enumerate(fields):
                    px1[c] = field

            @pl.when((step == steps - 1) & jnp.logical_not(even_x))
            def _():
                for c, field in enumerate(fields):
                    px2[c] = field

        mf = mask[i].astype(F32)
        for j in range(2):
            part = slice(128 * j, 128 * j + 128)
            m = mf[:, part]
            items = [(0, cd[:, part] * head[:, part] * m)]
            items += [(c + 1, sp[c, i, :, part] * m) for c in range(chans - 1)]
            items += [(7, m), (15, cd[:, part] * m)]
            acc = jnp.zeros((rows, 128), F32)
            for c, value in items:
                acc = jnp.where(lane == c, jnp.sum(value, axis=1, keepdims=True), acc)
            bsum[j, pl.ds(x * rows, rows), :] = acc

    @pl.when(step == steps - 1)
    def _():
        n_pipes = pa.shape[2]
        onehots = [block_onehot(bp[...], j, n_pipes) for j in range(2)]
        total = pipe_sums([bsum[0], bsum[1]], onehots, 16)
        small = obs[:, 0, :]
        wide = jnp.concatenate([small] * (n_pipes // small.shape[1]), axis=1)
        place = lax.broadcasted_iota(jnp.int32, wide.shape, 1) // small.shape[1]
        mine = jnp.where(place == gy, wide, 0.0)
        mine = jnp.concatenate([mine, jnp.zeros((1, n_pipes), F32)], axis=0)
        count = pa.shape[0] - 2
        pa[count] = total[:8]
        pa[count + 1] = total[8:] + mine
        pb[count] = total[:8]
        pb[count + 1] = total[8:] + mine


def first(h, sp, cond, cap, mask, bp, obs):
    nx, rows, depth = h.shape
    chans = sp.shape[0] + 1
    n_pipes = 256
    field = pl.BlockSpec((STEP, rows, depth), lambda i: (i, 0, 0))
    whole = lambda *shape: pl.BlockSpec(shape, lambda i: (0,) * len(shape))
    return pl.pallas_call(
        functools.partial(first_kernel, rows, chans),
        grid=(nx // STEP,),
        in_specs=[
            field,
            pl.BlockSpec((chans - 1, STEP, rows, depth), lambda i: (0, i, 0, 0)),
            field,
            field,
            field,
            whole(*bp.shape),
            whole(*obs.shape),
        ],
        out_specs=[
            field,
            whole(chans + 1, rows, depth),
            whole(chans + 1, rows, depth),
            whole(nx + 2, 8, n_pipes),
            whole(nx + 2, 8, n_pipes),
        ],
        out_shape=[
            jax.ShapeDtypeStruct((nx, rows, depth), F32),
            jax.ShapeDtypeStruct((chans + 1, rows, depth), F32),
            jax.ShapeDtypeStruct((chans + 1, rows, depth), F32),
            jax.ShapeDtypeStruct((nx + 2, 8, n_pipes), F32),
            jax.ShapeDtypeStruct((nx + 2, 8, n_pipes), F32),
        ],
        scratch_shapes=[pltpu.VMEM((2, nx * rows, 128), F32)],
        compiler_params=pltpu.CompilerParams(vmem_limit_bytes=32 * 2**20),
        cost_estimate=pl.CostEstimate(flops=10**7, bytes_accessed=8 * 10**6, transcendentals=0),
    )(h, sp, cond, cap, mask, bp, obs)


def step_kernel(k, last, nx, rows, chans, *refs):
    refs = list(refs)
    take = lambda n: [refs.pop(0) for _ in range(n)]
    diffusion, coupling, react = take(3)
    sums = take(k + 1)
    (bp,) = take(1)
    h, sh, sp, cond, cap, rate, mat, mask = take(8)
    xr1, xr2, yra, yrb = take(4)
    cx1, cx2, cya, cyb = (xr1, xr2, yra, yrb) if k == 0 else take(4)
    if last:
        oh, osp = take(2)
    else:
        oh, osh, osp, px1, px2, pa, pb = take(7)
    st, kc, vh, vcap, vrate, vmat, vmask = take(7)
    ya, yb = take(2)
    if k > 0:
        yca, ycb = take(2)
    else:
        yca, ycb = ya, yb
    th, tsh, tsp, hot, ansr, bsum = take(6)
    in_sem, halo_sem, out_sem = take(3)

    n_pipes = 256
    nsp = chans - 1
    even_x = lax.axis_index("gx") % 2 == 0
    gy = lax.axis_index("gy")
    even_y = gy % 2 == 0
    last_y = lax.axis_size("gy") - 1

    inside = pl.ds(TOP, rows)
    lanes = [pl.ds(0, 128), pl.ds(128, 128)]

    def chunk(g):
        at = pl.ds(g * STEP, STEP)
        into = pl.ds(g * STEP + 1, STEP)
        pairs = []
        for j in range(2):
            pairs.append((sh.at[at, :, lanes[j]], st.at[j, 0, into, inside, :]))
            pairs.append((sp.at[:, at, :, lanes[j]], st.at[j, pl.ds(1, nsp), into, inside, :]))
            pairs.append((cond.at[at, :, lanes[j]], kc.at[j, into, inside, :]))
        for src, dst in ((h, vh), (rate, vrate), (mat, vmat), (mask, vmask)):
            pairs.append((src.at[at], dst.at[at]))
        if not last:
            pairs.append((cap.at[at], vcap.at[at]))
        return [
            pltpu.make_async_copy(a, b, in_sem.at[g, n]) for n, (a, b) in enumerate(pairs)
        ]

    x1_at = jnp.where(even_x, nx + 1, 0)
    x2_at = jnp.where(even_x, 0, nx + 1)

    def halos():
        pairs = [(yra, ya), (yrb, yb)]
        if k > 0:
            pairs += [(cya, yca), (cyb, ycb)]
        for recv, crecv, at in ((xr1, cx1, x1_at), (xr2, cx2, x2_at)):
            for j in range(2):
                pairs.append(
                    (recv.at[pl.ds(0, chans), :, lanes[j]], st.at[j, :, at, inside, :])
                )
                pairs.append((crecv.at[chans, :, lanes[j]], kc.at[j, at, inside, :]))
        return [
            pltpu.make_async_copy(a, b, halo_sem.at[n]) for n, (a, b) in enumerate(pairs)
        ]

    for copy in chunk(0):
        copy.start()
    for copy in halos():
        copy.start()
    for g in range(1, nx // STEP):
        for copy in chunk(g):
            copy.start()

    t0 = sums[0]
    root = jnp.sqrt(t0[0, 7:8, :] + 1.0)
    observed = t0[1]
    row = lax.broadcasted_iota(jnp.int32, (8, n_pipes), 0)
    weight = drain_gain * jnp.where(row == 0, t0[1, 7:8, :], t0[0, 7:8, :])
    answer = jnp.tanh(observed - t0[0] / root)
    for later in sums[1:]:
        answer = jnp.tanh(observed - (later[0] + answer * weight) / root)
    tall = jnp.concatenate([drain_gain * answer, jnp.zeros((120, n_pipes), F32)], axis=0)
    pieces = split3(tall)
    for j in range(2):
        onehot = block_onehot(bp[...], j, n_pipes)
        hot[j] = onehot
        total = None
        for piece in pieces:
            part = lax.dot_general(
                onehot, piece, (((1,), (1,)), ((), ())), preferred_element_type=F32
            )
            total = part if total is None else total + part
        ansr[j] = total

    for copy in chunk(0):
        copy.wait()
    for copy in halos():
        copy.wait()

    lane = lax.broadcasted_iota(jnp.int32, (RB, 128), 1)
    first_lane, last_lane = lane == 0, lane == 127
    a_lo = jnp.where(even_y, 0.0, 1.0)
    b_lo = jnp.where(even_y & (gy > 0), 1.0, 0.0)
    a_hi = jnp.where(even_y, 1.0, 0.0)
    b_hi = jnp.where(even_y | (gy == last_y), 0.0, 1.0)

    def updown(pair):
        left = [pltpu.roll(v, 1, 1) for v in pair]
        right = [pltpu.roll(v, 127, 1) for v in pair]
        up = [jnp.where(first_lane, 0.0, left[0]), jnp.where(first_lane, left[0], left[1])]
        down = [jnp.where(last_lane, right[1], right[0]), jnp.where(last_lane, 0.0, right[1])]
        return up, down

    def plane(x, carry):
        @pl.when((x % STEP == STEP - 1) & (x < nx - 1))
        def _():
            for copy in chunk(x // STEP + 1):
                copy.wait()

        for j in range(2):
            va, vb = ya[x, :, 128 * j : 128 * j + 128], yb[x, :, 128 * j : 128 * j + 128]
            lo, hi = va * a_lo + vb * b_lo, va * a_hi + vb * b_hi
            for c in range(chans):
                st[j, c, x + 1, TOP - 1 : TOP, :] = lo[c : c + 1]
                st[j, c, x + 1, TOP + rows : TOP + rows + 1, :] = hi[c : c + 1]
            if k == 0:
                clo, chi = lo, hi
            else:
                va, vb = yca[x, :, 128 * j : 128 * j + 128], ycb[x, :, 128 * j : 128 * j + 128]
                clo, chi = va * a_lo + vb * b_lo, va * a_hi + vb * b_hi
            kc[j, x + 1, TOP - 1 : TOP, :] = clo[chans : chans + 1]
            kc[j, x + 1, TOP + rows : TOP + rows + 1, :] = chi[chans : chans + 1]

        edge = {}
        for r in range(0, rows, RB):
            at = TOP + r
            both = range(2)
            part = [slice(0, 128), slice(128, 256)]
            body = slice(r, r + RB)

            def sides(ref, *lead):
                out = []
                for j in both:
                    out.append(
                        [
                            ref[(j, *lead, x, slice(at, at + RB))],
                            ref[(j, *lead, x + 2, slice(at, at + RB))],
                            ref[(j, *lead, x + 1, slice(at - 1, at - 1 + RB))],
                            ref[(j, *lead, x + 1, slice(at + 1, at + 1 + RB))],
                        ]
                    )
                center = [ref[(j, *lead, x + 1, slice(at, at + RB))] for j in both]
                return center, out

            m = [vmask[x, body, part[j]].astype(F32) for j in both]
            rt = [time_step * vrate[x, body, part[j]] for j in both]
            mt = [vmat[x, body, part[j]] for j in both]
            odd = [v % 2 == 1 for v in mt]
            high = [v >= 2 for v in mt]
            ans = [ansr[j, pl.ds(x * rows + r, RB), :] for j in both]
            bacc = [jnp.zeros((RB, 128), F32) for _ in both]

            c_mid, c_near = sides(kc)
            s_mid, s_near = sides(st, 0)
            c_up, c_down = updown(c_mid)
            s_up, s_down = updown(s_mid)
            flow = []
            for j in both:
                acc = None
                near_c = c_near[j] + [c_up[j], c_down[j]]
                near_s = s_near[j] + [s_up[j], s_down[j]]
                for oc, os in zip(near_c, near_s):
                    term = (c_mid[j] + oc) * (os - s_mid[j])
                    acc = term if acc is None else acc + term
                flow.append(0.5 * acc)

            mids = []
            outs = [[None] * chans for _ in both]
            for c in range(nsp):
                mid, near = sides(st, c + 1)
                up, down = updown(mid)
                kd = time_step * diffusion[c]
                mids.append(mid)
                for j in both:
                    n4 = (near[j][0] + near[j][1]) + (near[j][2] + near[j][3])
                    n6 = n4 + (up[j] + down[j])
                    outs[j][c + 1] = mid[j] + kd * (n6 - 6.0 * mid[j])
            for j in both:
                source = None
                for c in range(nsp):
                    term = coupling[c] * mids[c][j]
                    source = term if source is None else source + term
                outs[j][0] = vh[x, body, part[j]] + flow[j] + rt[j] * source
            for s in range(nsp):
                acc = [None, None]
                for t in range(nsp):
                    r0, r1, r2, r3 = (react[i, t, s] for i in range(4))
                    for j in both:
                        w = jnp.where(
                            high[j], jnp.where(odd[j], r3, r2), jnp.where(odd[j], r1, r0)
                        )
                        term = w * mids[t][j]
                        acc[j] = term if acc[j] is None else acc[j] + term
                for j in both:
                    outs[j][s + 1] = outs[j][s + 1] - rt[j] * acc[j]
            for j in both:
                for c in range(chans):
                    value = outs[j][c]
                    if not last:
                        drained = value * m[j]
                        if c == 0:
                            drained = drained * c_mid[j]
                        bacc[j] = jnp.where(
                            lane == c, jnp.sum(drained, axis=1, keepdims=True), bacc[j]
                        )
                    value = value + m[j] * ans[j][:, c : c + 1]
                    if c == 0:
                        th[x, body, part[j]] = value
                        if last:
                            continue
                        value = time_step * value / vcap[x, body, part[j]]
                        tsh[x, body, part[j]] = value
                    else:
                        tsp[c - 1, x, body, part[j]] = value
                    if r == 0:
                        edge[j, c] = value[0:1]
                    if r == rows - RB and not last:
                        lo, hi = edge[j, c], value[RB - 1 : RB]
                        pa[x, c : c + 1, part[j]] = jnp.where(even_y, hi, lo)
                        pb[x, c : c + 1, part[j]] = jnp.where(even_y, lo, hi)
                if not last:
                    bsum[j, pl.ds(x * rows + r, RB), :] = bacc[j]

        @pl.when(x % STEP == STEP - 1)
        def _():
            for copy in result(x // STEP):
                copy.start()

        return carry

    def result(g):
        at = pl.ds(g * STEP, STEP)
        pairs = [(th.at[at], oh.at[at]), (tsp.at[:, at], osp.at[:, at])]
        if not last:
            pairs.append((tsh.at[at], osh.at[at]))
        return [
            pltpu.make_async_copy(a, b, out_sem.at[g, n]) for n, (a, b) in enumerate(pairs)
        ]

    lax.fori_loop(0, nx, plane, 0)

    if not last:

        def send(dst, x):
            dst[0] = tsh[x]
            for c in range(nsp):
                dst[c + 1] = tsp[c, x]

        @pl.when(even_x)
        def _():
            send(px1, nx - 1)
            send(px2, 0)

        @pl.when(jnp.logical_not(even_x))
        def _():
            send(px1, 0)
            send(px2, nx - 1)

        total = pipe_sums([bsum[0], bsum[1]], [hot[0], hot[1]], 8)
        pa[nx] = total
        pb[nx] = total
        for c in range(nx):
            pa[c, chans:8, :] = jnp.zeros((8 - chans, n_pipes), F32)
            pb[c, chans:8, :] = jnp.zeros((8 - chans, n_pipes), F32)
    for g in range(nx // STEP):
        for copy in result(g):
            copy.wait()


def step(k, diffusion, coupling, react, sums, bp, h, sh, sp, cond, cap, rate, mat, mask, near, near0):
    last = k == ITERS - 1
    nx, rows, depth = h.shape
    nsp = sp.shape[0]
    chans = nsp + 1
    n_pipes = 256
    args = [diffusion, coupling, react, *sums, bp, h, sh, sp, cond, cap, rate, mat, mask, *near]
    specs = [SM] * 3 + [VM] * (len(sums) + 1) + [ANY] * 12
    if k > 0:
        args += near0
        specs += [ANY] * 4
    shapes = [(nx, rows, depth), (nsp, nx, rows, depth)]
    out_specs = [ANY, ANY]
    if not last:
        shapes.insert(1, (nx, rows, depth))
        shapes += [(chans, rows, depth)] * 2 + [(nx + 1, 8, n_pipes)] * 2
        out_specs += [ANY] + [VM] * 4
    field = lambda dtype: pltpu.VMEM((nx, rows, depth), dtype)
    scratch = [
        pltpu.VMEM((2, chans, nx + 2, rows + 2 * TOP, 128), F32),
        pltpu.VMEM((2, nx + 2, rows + 2 * TOP, 128), F32),
        field(F32),
        field(F32),
        field(F32),
        field(jnp.int32),
        field(jnp.int32),
    ]
    scratch += [pltpu.VMEM(a.shape, F32) for a in (near[2:] + (near0[2:] if k > 0 else []))]
    scratch += [
        field(F32),
        field(F32),
        pltpu.VMEM((nsp, nx, rows, depth), F32),
        pltpu.VMEM((2, nx * rows, n_pipes), BF16),
        pltpu.VMEM((2, nx * rows, 128), F32),
        pltpu.VMEM((2, nx * rows, 128), F32),
        pltpu.SemaphoreType.DMA((nx // STEP, 11)),
        pltpu.SemaphoreType.DMA((12,)),
        pltpu.SemaphoreType.DMA((nx // STEP, 3)),
    ]
    return pl.pallas_call(
        functools.partial(step_kernel, k, last, nx, rows, chans),
        in_specs=specs,
        out_specs=out_specs,
        out_shape=[jax.ShapeDtypeStruct(s, F32) for s in shapes],
        scratch_shapes=scratch,
        compiler_params=pltpu.CompilerParams(vmem_limit_bytes=40 * 2**20),
        cost_estimate=pl.CostEstimate(
            flops=6 * 10**7, bytes_accessed=10**7, transcendentals=0
        ),
    )(*args)


def swap(x, axis, first_low):
    count = lax.axis_size(axis)
    pairs = []
    for low in range(first_low, count - 1, 2):
        pairs += [(low, low + 1), (low + 1, low)]
    return lax.ppermute(x, axis, pairs)


def exchange(px1, px2, pa, pb, nx):
    count = lax.axis_size("gy")
    x1 = swap(px1, "gx", 0)
    x2 = swap(px2, "gx", 1)
    ya = swap(pa, "gy", 0)
    pair_sum = pa[nx:] + ya[nx:]
    pb = lax.dynamic_update_slice(pb, pair_sum, (nx, 0, 0))
    ring = []
    for low in range(1, count, 2):
        other = (low + 1) % count
        ring += [(low, other), (other, low)]
    yb = lax.ppermute(pb, "gy", ring)
    four = pair_sum + yb[nx:]
    far = lax.ppermute(four, "gy", [(i, (i + count // 2) % count) for i in range(count)])
    return [x1, x2, ya, yb], four + far


def body(
    adj_head,
    adj_species,
    cond,
    capacity,
    rate,
    diffusion,
    coupling,
    react,
    material,
    drain_mask,
    block_pipe,
    pipe_obs,
):
    nx = adj_head.shape[0]
    h, sp = adj_head, adj_species
    sh, px1, px2, pa, pb = first(h, sp, cond, capacity, drain_mask, block_pipe, pipe_obs)
    near0 = None
    sums = []
    for k in range(ITERS):
        near, total = exchange(px1, px2, pa, pb, nx)
        near0 = near if k == 0 else near0
        sums.append(total)
        out = step(
            k, diffusion, coupling, react, sums, block_pipe, h, sh, sp, cond, capacity,
            rate, material, drain_mask, near, near0,
        )
        if k < ITERS - 1:
            h, sh, sp, px1, px2, pa, pb = out
        else:
            h, sp = out
    return (h, sp)


def solution(mesh):
    return jax.shard_map(
        body,
        mesh=mesh,
        in_specs=(
            P("gx", "gy", None),
            P(None, "gx", "gy", None),
            P("gx", "gy", None),
            P("gx", "gy", None),
            P("gx", "gy", None),
            P(),
            P(),
            P(),
            P("gx", "gy", None),
            P("gx", "gy", None),
            P("gx", "gy", None),
            P(None, "gx", "gy"),
        ),
        out_specs=(P("gx", "gy", None), P(None, "gx", "gy", None)),
        check_vma=False,
    )
```

```python
import functools

import jax
import jax.numpy as jnp
from jax import lax
from jax.experimental import pallas as pl
from jax.experimental.pallas import tpu as pltpu
from jax.sharding import PartitionSpec as P

ITERS = 3
time_step = 0.08
drain_gain = 0.5

F32 = jnp.float32
BF16 = jnp.bfloat16
HB = pl.BlockSpec(memory_space=pltpu.HBM)
ANY = pl.BlockSpec(memory_space=pl.ANY)
VM = pl.BlockSpec(memory_space=pltpu.VMEM)
SM = pl.BlockSpec(memory_space=pltpu.SMEM)
TOP = 8
STEP = 4
RB = 16


VLIM = 18 * 2**20
LANES = (slice(0, 128), slice(128, 256))


def split(x, pieces):
    out = []
    for _ in range(pieces):
        piece = x.astype(BF16)
        out.append(piece)
        x = x - piece.astype(F32)
    return out


def block_onehot(bp, block, n_pipes):
    col = bp[:, :, block : block + 1]
    col = col.reshape(col.shape[0] * col.shape[1], 1)
    return (col == lax.broadcasted_iota(jnp.int32, (col.shape[0], n_pipes), 1)).astype(BF16)


def turn(x, by):
    return pltpu.roll(x, (-by) % 128, 1)


def halve(values):
    low = lax.broadcasted_iota(jnp.int32, values[0].shape, 1) < 64
    return [
        jnp.where(low, a, b) + turn(jnp.where(low, b, a), 64)
        for a, b in zip(values[::2], values[1::2])
    ]


def merge(level):
    lane = lax.broadcasted_iota(jnp.int32, level[0].shape, 1)
    for width in (32, 16):
        low = lane & width == 0
        level = [
            jnp.where(low, a, b) + jnp.where(low, turn(a, width), turn(b, -width))
            for a, b in zip(level[::2], level[1::2])
        ]
    return level[0]


SUM_LANE = [64 * (c & 1) + 32 * (c >> 1 & 1) + 16 * (c >> 2 & 1) for c in range(8)]
CHUNK = 128


def block_sums(half, j):
    lane = lax.broadcasted_iota(jnp.int32, (16, 128), 1) // 16
    chan = lax.broadcasted_iota(jnp.int32, (16, 128), 0)
    group = 4 * (chan & 1) + 2 * (chan >> 1 & 1) + (chan >> 2 & 1)
    pick = ((lane == group) & (chan < 8)).astype(BF16)
    out = []
    for r in range(0, half.shape[2], CHUNK):
        merged = merge([half[j, c, r : r + CHUNK, :] for c in range(4)])
        total = None
        for piece in split(merged, 3)[::-1]:
            part = lax.dot_general(
                pick, piece, (((1,), (1,)), ((), ())), preferred_element_type=F32
            )
            total = part if total is None else total + part
        out.append(total)
    return jnp.concatenate(out, axis=1)[:8]


def pipe_sums(half, hot):
    total = None
    for j in range(2):
        rows = block_sums(half, j)
        stack = jnp.concatenate(split(rows, 3) + [jnp.zeros(rows.shape, BF16)], axis=0)
        part = jnp.dot(stack, hot[j], preferred_element_type=F32)
        total = part if total is None else total + part
    return (total[16:24] + total[8:16]) + total[:8]


def edge_flags():
    gx, gy = lax.axis_index("gx"), lax.axis_index("gy")
    return gx % 2 == 0, gy % 2 == 0, gy


def edges(h, sp, cond, cap):
    nx = h.shape[0]
    even = lax.axis_index("gx") % 2 == 0

    def pack(x):
        plane = lambda a, dim: lax.dynamic_slice_in_dim(a, x, 1, axis=dim)
        scaled = time_step * plane(h, 0) / plane(cap, 0)
        return jnp.concatenate([scaled, plane(sp, 1)[:, 0], plane(cond, 0)], axis=0)

    return pack(jnp.where(even, nx - 1, 0)), pack(jnp.where(even, 0, nx - 1))


def clear_rim(ref, nx, rows, *lead):
    tile = jnp.zeros((TOP, 128), F32)
    for j in range(2):
        for x in (0, nx + 1):
            for r in range(0, rows + 2 * TOP, TOP):
                ref[(j, *lead, x, slice(r, r + TOP))] = tile


def first_kernel(
    nx, rows, chans, h, sp, cond, cap, mask, bp, obs, st, kc, pa, pb, hot, half, whalf, vh, vcap, vmask, sem
):
    _, even_y, gy = edge_flags()
    nsp = chans - 1
    n_pipes = pa.shape[2]
    inside = pl.ds(TOP, rows)

    def chunk(g):
        at, into = pl.ds(g * STEP, STEP), pl.ds(g * STEP + 1, STEP)
        pairs = []
        for j in range(2):
            part = pl.ds(128 * j, 128)
            pairs.append((sp.at[:, at, :, part], st.at[j, pl.ds(1, nsp), into, inside, :]))
            pairs.append((cond.at[at, :, part], kc.at[j, into, inside, :]))
        for src, dst in ((h, vh), (cap, vcap), (mask, vmask)):
            pairs.append((src.at[at], dst.at[at]))
        return [pltpu.make_async_copy(a, b, sem.at[g, n]) for n, (a, b) in enumerate(pairs)]

    for g in range(nx // STEP):
        for copy in chunk(g):
            copy.start()
    for j in range(2):
        hot[j] = block_onehot(bp[...], j, n_pipes)
    for c in range(chans):
        clear_rim(st, nx, rows, c)
    clear_rim(kc, nx, rows)
    rim = jnp.zeros((TOP, 128), F32)
    low = lax.broadcasted_iota(jnp.int32, (rows, 128), 1) < 64

    def plane(x, carry):
        @pl.when(x % STEP == 0)
        def _():
            for copy in chunk(x // STEP):
                copy.wait()

        for j, part in enumerate(LANES):
            cd = kc[j, x + 1, TOP : TOP + rows, :]
            head = vh[x, :, part]
            m = vmask[x, :, part].astype(F32)
            scaled = time_step * head / vcap[x, :, part]
            st[j, 0, x + 1, TOP : TOP + rows, :] = scaled
            species = [st[j, c, x + 1, TOP : TOP + rows, :] for c in range(1, chans)]
            for c in range(chans):
                st[j, c, x + 1, 0:TOP, :] = rim
                st[j, c, x + 1, TOP + rows : 2 * TOP + rows, :] = rim
            kc[j, x + 1, 0:TOP, :] = rim
            kc[j, x + 1, TOP + rows : 2 * TOP + rows, :] = rim
            for c, field in enumerate([scaled, *species, cd]):
                lo, hi = field[0:1], field[rows - 1 : rows]
                pa[x, c : c + 1, part] = jnp.where(even_y, hi, lo)
                pb[x, c : c + 1, part] = jnp.where(even_y, lo, hi)
            weight = cd * m
            sums = halve([weight * head] + [v * m for v in species] + [m])
            place = pl.ds(x * rows, rows)
            for c in range(4):
                half[j, c, place, :] = sums[c]
            whalf[j, 0, place, :] = jnp.where(low, weight + turn(weight, 64), 0.0)
            for c in range(1, 4):
                whalf[j, c, place, :] = jnp.zeros_like(weight)
        return carry

    lax.fori_loop(0, nx, plane, 0)
    total = pipe_sums(half, hot)
    total_w = pipe_sums(whalf, hot)
    small = obs[:, 0, :]
    wide = jnp.concatenate([small] * (n_pipes // small.shape[1]), axis=1)
    place = lax.broadcasted_iota(jnp.int32, wide.shape, 1) // small.shape[1]
    mine = jnp.where(place == gy, wide, 0.0)
    second = jnp.concatenate([mine, total_w[:1]], axis=0)
    for dst in (pa, pb):
        dst[nx] = total
        dst[nx + 1] = second


def first(h, sp, cond, cap, mask, bp, obs):
    nx, rows, depth = h.shape
    chans = sp.shape[0] + 1
    n_pipes = 256
    shape = lambda *dims: jax.ShapeDtypeStruct(dims, F32)
    return pl.pallas_call(
        functools.partial(first_kernel, nx, rows, chans),
        in_specs=[HB] * 5 + [VM] * 2,
        out_specs=[VM] * 5,
        out_shape=[
            shape(2, chans, nx + 2, rows + 2 * TOP, 128),
            shape(2, nx + 2, rows + 2 * TOP, 128),
            shape(nx + 2, 8, n_pipes),
            shape(nx + 2, 8, n_pipes),
            jax.ShapeDtypeStruct((2, nx * rows, n_pipes), BF16),
        ],
        scratch_shapes=[
            pltpu.VMEM((2, 4, nx * rows, 128), F32),
            pltpu.VMEM((2, 4, nx * rows, 128), F32),
            pltpu.VMEM((nx, rows, depth), F32),
            pltpu.VMEM((nx, rows, depth), F32),
            pltpu.VMEM((nx, rows, depth), jnp.int32),
            pltpu.SemaphoreType.DMA((nx // STEP, 7)),
        ],
        compiler_params=pltpu.CompilerParams(vmem_limit_bytes=VLIM),
        cost_estimate=pl.CostEstimate(flops=10**7, bytes_accessed=8 * 10**6, transcendentals=0),
    )(h, sp, cond, cap, mask, bp, obs)


def inner_kernel(nx, rows, chans, diffusion, coupling, react, st, kc, h, rate, mat, out):
    nsp = chans - 1
    both = range(2)
    lane = lax.broadcasted_iota(jnp.int32, (RB, 128), 1)
    first_lane, last_lane = lane == 0, lane == 127

    def updown(pair):
        left = [turn(v, -1) for v in pair]
        right = [turn(v, 1) for v in pair]
        up = [jnp.where(first_lane, 0.0, left[0]), jnp.where(first_lane, left[0], left[1])]
        down = [jnp.where(last_lane, right[1], right[0]), jnp.where(last_lane, 0.0, right[1])]
        return up, down

    def plane(x, carry):
        for r in range(0, rows, RB):
            at = TOP + r
            body = slice(r, r + RB)

            def sides(ref, *lead):
                near = [
                    [
                        ref[(j, *lead, x, slice(at, at + RB))],
                        ref[(j, *lead, x + 2, slice(at, at + RB))],
                        ref[(j, *lead, x + 1, slice(at - 1, at - 1 + RB))],
                        ref[(j, *lead, x + 1, slice(at + 1, at + 1 + RB))],
                    ]
                    for j in both
                ]
                return [ref[(j, *lead, x + 1, slice(at, at + RB))] for j in both], near

            rt = [time_step * rate[x, body, LANES[j]] for j in both]
            mt = [mat[x, body, LANES[j]] for j in both]
            odd = [v % 2 == 1 for v in mt]
            high = [v >= 2 for v in mt]

            c_mid, c_near = sides(kc)
            s_mid, s_near = sides(st, 0)
            c_up, c_down = updown(c_mid)
            s_up, s_down = updown(s_mid)
            flow = []
            for j in both:
                acc = None
                near_c = c_near[j] + [c_up[j], c_down[j]]
                near_s = s_near[j] + [s_up[j], s_down[j]]
                for oc, os in zip(near_c, near_s):
                    term = (c_mid[j] + oc) * (os - s_mid[j])
                    acc = term if acc is None else acc + term
                flow.append(0.5 * acc)
            mids = []
            outs = [[None] * chans for _ in both]
            for c in range(nsp):
                mid, near = sides(st, c + 1)
                up, down = updown(mid)
                kd = time_step * diffusion[c]
                mids.append(mid)
                for j in both:
                    n4 = (near[j][0] + near[j][1]) + (near[j][2] + near[j][3])
                    n6 = n4 + (up[j] + down[j])
                    outs[j][c + 1] = mid[j] + kd * (n6 - 6.0 * mid[j])
            for j in both:
                source = None
                for c in range(nsp):
                    term = coupling[c] * mids[c][j]
                    source = term if source is None else source + term
                head = h[j, x, body] if len(h.shape) == 4 else h[x, body, LANES[j]]
                out[j, 0, x, body, :] = head + flow[j] + rt[j] * source
            for s in range(nsp):
                acc = [None, None]
                for t in range(nsp):
                    r0, r1, r2, r3 = (react[i, t, s] for i in range(4))
                    for j in both:
                        w = jnp.where(
                            high[j], jnp.where(odd[j], r3, r2), jnp.where(odd[j], r1, r0)
                        )
                        term = w * mids[t][j]
                        acc[j] = term if acc[j] is None else acc[j] + term
                for j in both:
                    out[j, s + 1, x, body, :] = outs[j][s + 1] - rt[j] * acc[j]
        return carry

    lax.fori_loop(0, nx, plane, 0)


def inner(diffusion, coupling, react, st, kc, h, rate, mat):
    nx, rows, depth = rate.shape
    chans = st.shape[1]
    return pl.pallas_call(
        functools.partial(inner_kernel, nx, rows, chans),
        in_specs=[SM] * 3 + [VM] * 5,
        out_specs=VM,
        out_shape=jax.ShapeDtypeStruct((2, chans, nx, rows, 128), F32),
        compiler_params=pltpu.CompilerParams(vmem_limit_bytes=VLIM),
        cost_estimate=pl.CostEstimate(flops=6 * 10**7, bytes_accessed=10**7, transcendentals=0),
    )(diffusion, coupling, react, st, kc, h, rate, mat)


def close_kernel(k, last, nx, rows, chans, *refs):
    refs = list(refs)
    take = lambda n: [refs.pop(0) for _ in range(n)]
    (diffusion,) = take(1)
    sums = take(k + 1)
    hot, inn, st, kc, cap, mask = take(6)
    xr1, xr2, ya, yb = take(4)
    cx1, cx2, cya, cyb = (xr1, xr2, ya, yb) if k == 0 else take(4)
    if last:
        oh, osp = take(2)
    else:
        oh, ost, px1, px2, pa, pb = take(6)
    ansb, half, xh = take(3)
    if last:
        th, tsp, sem = take(3)

    n_pipes = 256
    nsp = chans - 1
    even_x, even_y, gy = edge_flags()
    last_y = lax.axis_size("gy") - 1

    t0 = sums[0]
    root = jnp.sqrt(t0[0, 7:8, :] + 1.0)
    observed = t0[1]
    row = lax.broadcasted_iota(jnp.int32, (8, n_pipes), 0)
    weight = drain_gain * jnp.where(row == 0, t0[1, 7:8, :], t0[0, 7:8, :])
    answer = jnp.tanh(observed - t0[0] / root)
    for later in sums[1:]:
        answer = jnp.tanh(observed - (later[0] + answer * weight) / root)
    answer = drain_gain * answer
    tall = jnp.transpose(jnp.concatenate([answer, jnp.zeros((120, n_pipes), F32)], axis=0))
    pieces = jnp.concatenate(split(tall, 2), axis=1)
    part_of = lax.broadcasted_iota(jnp.int32, (256, 256), 1) // 128
    chan_of = lax.broadcasted_iota(jnp.int32, (256, 256), 0) % 128
    for j in range(2):
        picked = jnp.dot(hot[j], pieces, preferred_element_type=F32).astype(BF16)
        for c in range(0, chans, 2):
            spread = (part_of + c == chan_of).astype(BF16)
            wide = jnp.dot(picked, spread, preferred_element_type=F32)
            ansb[j, c] = wide[:, :128]
            if c + 1 < chans:
                ansb[j, c + 1] = wide[:, 128:]

    a_lo = jnp.where(even_y, 0.0, 1.0)
    b_lo = jnp.where(even_y & (gy > 0), 1.0, 0.0)
    a_hi = jnp.where(even_y, 1.0, 0.0)
    b_hi = jnp.where(even_y | (gy == last_y), 0.0, 1.0)
    row = lax.broadcasted_iota(jnp.int32, (8, 128), 0)
    top, bottom = row == 0, row == 7
    gains = jnp.zeros((8, 128), F32)
    for c in range(nsp):
        gains = jnp.where(row == c + 1, time_step * diffusion[c], gains)
    rim = jnp.zeros((TOP, 128), F32)
    if not last:
        for c in range(chans):
            clear_rim(ost, nx, rows, c)

    def pull(c_mid, s_mid, c_far, s_far):
        return 0.5 * ((c_mid + c_far) * s_far - c_far * s_mid)

    def keep(n, near, cnear):
        for c in range(chans):
            xh[n, c] = near[c]
        xh[n, chans] = cnear[chans]

    @pl.when(even_x)
    def _():
        keep(0, xr2, cx2)
        keep(1, xr1, cx1)

    @pl.when(jnp.logical_not(even_x))
    def _():
        keep(0, xr1, cx1)
        keep(1, xr2, cx2)

    def work(x, rim_at):
        for j, part in enumerate(LANES):
            def rims_of(ra, rb, wa, wb):
                return ra[x, :, part] * wa + rb[x, :, part] * wb

            m = mask[x, :, part].astype(F32)
            c_all = kc[j, x + 1, TOP : TOP + rows, :]
            add = []
            for at, wa, wb in ((0, a_lo, b_lo), (rows - 1, a_hi, b_hi)):
                far = rims_of(ya, yb, wa, wb)
                c_far = far if k == 0 else rims_of(cya, cyb, wa, wb)
                c_far = c_far[chans : chans + 1]
                s_mid = st[j, 0, x + 1, TOP + at : TOP + at + 1, :]
                head = pull(kc[j, x + 1, TOP + at : TOP + at + 1, :], s_mid, c_far, far[0:1])
                add.append((head, gains * far))
            values = []
            for c in range(chans):
                v = inn[j, c, x]
                lo, hi = ((a[0] if c == 0 else a[1][c : c + 1]) for a in add)
                v = jnp.concatenate(
                    [
                        v[:8] + jnp.where(top, lo, 0.0),
                        v[8 : rows - 8],
                        v[rows - 8 :] + jnp.where(bottom, hi, 0.0),
                    ],
                    axis=0,
                )
                if rim_at is not None:
                    far = xh[rim_at, c, :, part]
                    if c == 0:
                        s_all = st[j, 0, x + 1, TOP : TOP + rows, :]
                        v = v + pull(c_all, s_all, xh[rim_at, chans, :, part], far)
                    else:
                        v = v + time_step * diffusion[c - 1] * far
                values.append(v)
            if not last:
                drained = [v * m for v in values]
                drained[0] = drained[0] * c_all
                drained.append(jnp.zeros_like(m))
                for c, v in enumerate(halve(drained)):
                    half[j, c, pl.ds(x * rows, rows), :] = v
            for c, v in enumerate(values):
                v = v + m * ansb[j, c, pl.ds(x * rows, rows), :]
                if last:
                    if c == 0:
                        th[x, :, part] = v
                    else:
                        tsp[c - 1, x, :, part] = v
                    continue
                if c == 0:
                    oh[j, x] = v
                    v = time_step * v / cap[x, :, part]
                ost[j, c, x + 1, TOP : TOP + rows, :] = v
                ost[j, c, x + 1, 0:TOP, :] = rim
                ost[j, c, x + 1, TOP + rows : 2 * TOP + rows, :] = rim
                lo, hi = v[0:1], v[rows - 1 : rows]
                pa[x, c : c + 1, part] = jnp.where(even_y, hi, lo)
                pb[x, c : c + 1, part] = jnp.where(even_y, lo, hi)

    def result(g):
        at = pl.ds(g * STEP, STEP)
        pairs = [(th.at[at], oh.at[at]), (tsp.at[:, at], osp.at[:, at])]
        return [pltpu.make_async_copy(a, b, sem.at[g, n]) for n, (a, b) in enumerate(pairs)]

    def planes(i, carry):
        x = 2 * i
        work(x - 1, None)
        if last:

            @pl.when(x % STEP == 0)
            def _():
                for copy in result(x // STEP - 1):
                    copy.start()

        work(x, None)
        return carry

    def rim_plane(n, carry):
        work(n * (nx - 1), n)
        return carry

    lax.fori_loop(0, 2, rim_plane, 0)
    lax.fori_loop(1, nx // 2, planes, 0)
    if not last:

        def send(dst, x):
            for c in range(chans):
                for j, part in enumerate(LANES):
                    dst[c, :, part] = ost[j, c, x + 1, TOP : TOP + rows, :]

        @pl.when(even_x)
        def _():
            send(px1, nx - 1)
            send(px2, 0)

        @pl.when(jnp.logical_not(even_x))
        def _():
            send(px1, 0)
            send(px2, nx - 1)

        total = pipe_sums(half, hot)
        pa[nx] = total
        pb[nx] = total
    else:
        for copy in result(nx // STEP - 1):
            copy.start()
        for g in range(nx // STEP):
            for copy in result(g):
                copy.wait()


def close(k, diffusion, sums, hot, inn, st, kc, cap, mask, near, near0):
    last = k == ITERS - 1
    nx, rows, depth = cap.shape
    chans = st.shape[1]
    n_pipes = 256
    args = [diffusion, *sums, hot, inn, st, kc, cap, mask, *near]
    if k > 0:
        args += near0
    shape = lambda *dims: jax.ShapeDtypeStruct(dims, F32)
    scratch = [
        pltpu.VMEM((2, chans, nx * rows, 128), F32),
        pltpu.VMEM((2, 4, nx * rows, 128), F32),
        pltpu.VMEM((2, chans + 1, rows, depth), F32),
    ]
    if last:
        shapes = [shape(nx, rows, depth), shape(chans - 1, nx, rows, depth)]
        out_specs = [HB] * 2
        scratch += [
            pltpu.VMEM((nx, rows, depth), F32),
            pltpu.VMEM((chans - 1, nx, rows, depth), F32),
            pltpu.SemaphoreType.DMA((nx // STEP, 2)),
        ]
    else:
        shapes = [shape(2, nx, rows, 128), shape(*st.shape)]
        shapes += [shape(chans, rows, depth)] * 2 + [shape(nx + 1, 8, n_pipes)] * 2
        out_specs = [VM] * 6
    return pl.pallas_call(
        functools.partial(close_kernel, k, last, nx, rows, chans),
        in_specs=[SM] + [VM] * (len(args) - 1),
        out_specs=out_specs,
        out_shape=shapes,
        scratch_shapes=scratch,
        compiler_params=pltpu.CompilerParams(vmem_limit_bytes=VLIM),
        cost_estimate=pl.CostEstimate(flops=2 * 10**7, bytes_accessed=10**7, transcendentals=0),
    )(*args)


def swap(x, axis, first_low):
    count = lax.axis_size(axis)
    pairs = []
    for low in range(first_low, count - 1, 2):
        pairs += [(low, low + 1), (low + 1, low)]
    return lax.ppermute(x, axis, pairs)


def beside_x(px1, px2):
    return [swap(px1, "gx", 0), swap(px2, "gx", 1)]


def beside_y(pa, pb, nx):
    count = lax.axis_size("gy")
    ya = swap(pa, "gy", 0)
    pair_sum = pa[nx:] + ya[nx:]
    pb = lax.dynamic_update_slice(pb, pair_sum, (nx, 0, 0))
    ring = []
    for low in range(1, count, 2):
        other = (low + 1) % count
        ring += [(low, other), (other, low)]
    yb = lax.ppermute(pb, "gy", ring)
    four = pair_sum + yb[nx:]
    far = lax.ppermute(four, "gy", [(i, (i + count // 2) % count) for i in range(count)])
    return [ya, yb], four + far


def body(
    adj_head,
    adj_species,
    cond,
    capacity,
    rate,
    diffusion,
    coupling,
    react,
    material,
    drain_mask,
    block_pipe,
    pipe_obs,
):
    nx = adj_head.shape[0]
    packs = edges(adj_head, adj_species, cond, capacity)
    near_x = beside_x(*packs)
    block_pipe, _ = lax.optimization_barrier((block_pipe, packs))
    st, kc, pa, pb, hot = first(
        adj_head, adj_species, cond, capacity, drain_mask, block_pipe, pipe_obs
    )
    h = adj_head
    near0 = None
    sums = []
    for k in range(ITERS):
        near_y, total = beside_y(pa, pb, nx)
        near = near_x + near_y
        near0 = near if k == 0 else near0
        sums.append(total)
        inn = inner(diffusion, coupling, react, st, kc, h, rate, material)
        out = close(k, diffusion, sums, hot, inn, st, kc, capacity, drain_mask, near, near0)
        if k < ITERS - 1:
            h, st, px1, px2, pa, pb = out
            near_x = beside_x(px1, px2)
    return tuple(out)


def solution(mesh):
    return jax.shard_map(
        body,
        mesh=mesh,
        in_specs=(
            P("gx", "gy", None),
            P(None, "gx", "gy", None),
            P("gx", "gy", None),
            P("gx", "gy", None),
            P("gx", "gy", None),
            P(),
            P(),
            P(),
            P("gx", "gy", None),
            P("gx", "gy", None),
            P("gx", "gy", None),
            P(None, "gx", "gy"),
        ),
        out_specs=(P("gx", "gy", None), P(None, "gx", "gy", None)),
        check_vma=False,
    )
```

```python
import functools

import jax
import jax.numpy as jnp
from jax import lax
from jax.experimental import pallas as pl
from jax.experimental.pallas import tpu as pltpu
from jax.sharding import PartitionSpec as P

ITERS = 3
time_step = 0.08
drain_gain = 0.5

F32 = jnp.float32
BF16 = jnp.bfloat16
HB = pl.BlockSpec(memory_space=pltpu.HBM)
ANY = pl.BlockSpec(memory_space=pl.ANY)
VM = pl.BlockSpec(memory_space=pltpu.VMEM)
SM = pl.BlockSpec(memory_space=pltpu.SMEM)
TOP = 8
STEP = 4
RB = 16


VLIM = 14 * 2**20
LANES = (slice(0, 128), slice(128, 256))


def split(x, pieces):
    out = []
    for _ in range(pieces):
        piece = x.astype(BF16)
        out.append(piece)
        x = x - piece.astype(F32)
    return out


def block_onehots(bp, hot):
    nx, blocks, rows = bp.shape
    n_pipes = hot.shape[2]
    flat = bp[...].astype(F32).reshape(nx * blocks, rows)
    flat = jnp.concatenate([flat, jnp.zeros((128 - nx * blocks, rows), F32)], axis=0)
    tall = jnp.transpose(jnp.concatenate([flat, jnp.zeros((128, 128 - rows), F32)], axis=1))
    pipe = lax.broadcasted_iota(jnp.int32, (rows, n_pipes), 1).astype(F32)
    for x in range(nx):
        for j in range(blocks):
            n = x * blocks + j
            match = tall[:rows, n : n + 1] == pipe
            hot[j, x * rows : (x + 1) * rows, :] = match.astype(BF16)


def turn(x, by):
    return pltpu.roll(x, (-by) % 128, 1)


def halve(values):
    low = lax.broadcasted_iota(jnp.int32, values[0].shape, 1) < 64
    return [
        jnp.where(low, a, b) + turn(jnp.where(low, b, a), 64)
        for a, b in zip(values[::2], values[1::2])
    ]


def merge(level):
    lane = lax.broadcasted_iota(jnp.int32, level[0].shape, 1)
    for width in (32, 16):
        low = lane & width == 0
        level = [
            jnp.where(low, a, b) + jnp.where(low, turn(a, width), turn(b, -width))
            for a, b in zip(level[::2], level[1::2])
        ]
    return level[0]


SUM_LANE = [64 * (c & 1) + 32 * (c >> 1 & 1) + 16 * (c >> 2 & 1) for c in range(8)]
CHUNK = 128


def block_sums(half, j):
    lane = lax.broadcasted_iota(jnp.int32, (16, 128), 1) // 16
    chan = lax.broadcasted_iota(jnp.int32, (16, 128), 0)
    group = 4 * (chan & 1) + 2 * (chan >> 1 & 1) + (chan >> 2 & 1)
    pick = ((lane == group) & (chan < 8)).astype(BF16)
    out = []
    for r in range(0, half.shape[2], CHUNK):
        merged = merge([half[j, c, r : r + CHUNK, :] for c in range(4)])
        total = None
        for piece in split(merged, 3)[::-1]:
            part = lax.dot_general(
                pick, piece, (((1,), (1,)), ((), ())), preferred_element_type=F32
            )
            total = part if total is None else total + part
        out.append(total)
    return jnp.concatenate(out, axis=1)[:8]


def pipe_sums(half, hot):
    total = None
    for j in range(2):
        rows = block_sums(half, j)
        stack = jnp.concatenate(split(rows, 3) + [jnp.zeros(rows.shape, BF16)], axis=0)
        part = jnp.dot(stack, hot[j], preferred_element_type=F32)
        total = part if total is None else total + part
    return (total[16:24] + total[8:16]) + total[:8]


def edge_flags():
    gx, gy = lax.axis_index("gx"), lax.axis_index("gy")
    return gx % 2 == 0, gy % 2 == 0, gy


def clear_rim(ref, nx, rows, *lead):
    tile = jnp.zeros((TOP, 128), F32)
    for j in range(2):
        for x in (0, nx + 1):
            for r in range(0, rows + 2 * TOP, TOP):
                ref[(j, *lead, x, slice(r, r + TOP))] = tile


def first_kernel(
    nx, rows, chans, h, sp, cond, cap, mask, bp, obs, px1, px2, pa, pb, hot,
    half, vh, vs, vk, vcap, vmask, sem, tiny_sem, vbp, vobs
):
    even_x, even_y, gy = edge_flags()
    n_pipes = pa.shape[2]

    def chunk(g):
        at = pl.ds(g * STEP, STEP)
        pairs = [(sp.at[:, at], vs.at[:, at])]
        for src, dst in ((h, vh), (cond, vk), (cap, vcap), (mask, vmask)):
            pairs.append((src.at[at], dst.at[at]))
        return [pltpu.make_async_copy(a, b, sem.at[g, n]) for n, (a, b) in enumerate(pairs)]

    tiny = [pltpu.make_async_copy(bp, vbp, tiny_sem.at[0]), pltpu.make_async_copy(obs, vobs, tiny_sem.at[1])]
    for copy in tiny:
        copy.start()
    for g in range(nx // STEP):
        for copy in chunk(g):
            copy.start()
    for copy in tiny:
        copy.wait()
    block_onehots(vbp, hot)

    def planes(i, carry):
        @pl.when(i % (STEP // 2) == 0)
        def _():
            for copy in chunk(i // (STEP // 2)):
                copy.wait()

        work(2 * i)
        work(2 * i + 1)
        return carry

    def work(x):
        for j, part in enumerate(LANES):
            cd = vk[x, :, part]
            head = vh[x, :, part]
            m = vmask[x, :, part].astype(F32)
            scaled = time_step * head / vcap[x, :, part]
            species = [vs[c, x, :, part] for c in range(chans - 1)]
            for c, field in enumerate([scaled, *species, cd]):
                lo, hi = field[0:1], field[rows - 1 : rows]
                pa[x, c : c + 1, part] = jnp.where(even_y, hi, lo)
                pb[x, c : c + 1, part] = jnp.where(even_y, lo, hi)
            sums = halve([cd * m * head] + [v * m for v in species] + [m])
            place = pl.ds(x * rows, rows)
            for c in range(4):
                half[j, c, place, :] = sums[c]

    lax.fori_loop(0, nx // 2, planes, 0)

    def send(dst, x):
        dst[0] = time_step * vh[x] / vcap[x]
        for c in range(chans - 1):
            dst[c + 1] = vs[c, x]
        dst[chans] = vk[x]

    @pl.when(even_x)
    def _():
        send(px1, nx - 1)
        send(px2, 0)

    @pl.when(jnp.logical_not(even_x))
    def _():
        send(px1, 0)
        send(px2, nx - 1)

    total = pipe_sums(half, hot)
    small = vobs[:, 0, :]
    wide = jnp.concatenate([small] * (n_pipes // small.shape[1]), axis=1)
    place = lax.broadcasted_iota(jnp.int32, wide.shape, 1) // small.shape[1]
    mine = jnp.where(place == gy, wide, 0.0)
    second = jnp.concatenate([mine, jnp.zeros((1, n_pipes), F32)], axis=0)
    for dst in (pa, pb):
        dst[nx] = total
        dst[nx + 1] = second


def first(h, sp, cond, cap, mask, bp, obs):
    nx, rows, depth = h.shape
    chans = sp.shape[0] + 1
    n_pipes = 256
    shape = lambda *dims: jax.ShapeDtypeStruct(dims, F32)
    field = lambda dtype: pltpu.VMEM((nx, rows, depth), dtype)
    return pl.pallas_call(
        functools.partial(first_kernel, nx, rows, chans),
        in_specs=[HB] * 7,
        out_specs=[VM] * 5,
        out_shape=[
            shape(chans + 1, rows, depth),
            shape(chans + 1, rows, depth),
            shape(nx + 2, 8, n_pipes),
            shape(nx + 2, 8, n_pipes),
            jax.ShapeDtypeStruct((2, nx * rows, n_pipes), BF16),
        ],
        scratch_shapes=[
            pltpu.VMEM((2, 4, nx * rows, 128), F32),
            field(F32),
            pltpu.VMEM(sp.shape, F32),
            field(F32),
            field(F32),
            field(jnp.int32),
            pltpu.SemaphoreType.DMA((nx // STEP, 5)),
            pltpu.SemaphoreType.DMA((2,)),
            pltpu.VMEM(bp.shape, jnp.int32),
            pltpu.VMEM(obs.shape, F32),
        ],
        compiler_params=pltpu.CompilerParams(vmem_limit_bytes=53 * 2**20),
        cost_estimate=pl.CostEstimate(flops=10**7, bytes_accessed=8 * 10**6, transcendentals=0),
    )(h, sp, cond, cap, mask, bp, obs)


def inner_kernel(fresh, nx, rows, chans, diffusion, coupling, react, rate, h, *refs):
    if fresh:
        mat, cap, sp, cond, coef, kc, out, st, vh, vcap, sem = refs
    else:
        coef, kc, st, out = refs
    nsp = chans - 1
    both = range(2)
    lane = lax.broadcasted_iota(jnp.int32, (RB, 128), 1)
    first_lane, last_lane = lane == 0, lane == 127

    def updown(pair):
        left = [turn(v, -1) for v in pair]
        right = [turn(v, 1) for v in pair]
        up = [jnp.where(first_lane, 0.0, left[0]), jnp.where(first_lane, left[0], left[1])]
        down = [jnp.where(last_lane, right[1], right[0]), jnp.where(last_lane, 0.0, right[1])]
        return up, down

    def chunk(g):
        at, into = pl.ds(g * STEP, STEP), pl.ds(g * STEP + 1, STEP)
        inside = pl.ds(TOP, rows)
        pairs = []
        for j, part in enumerate((pl.ds(0, 128), pl.ds(128, 128))):
            pairs.append((sp.at[:, at, :, part], st.at[j, pl.ds(1, nsp), into, inside, :]))
            pairs.append((cond.at[at, :, part], kc.at[j, into, inside, :]))
        for src, dst in ((h, vh), (cap, vcap)):
            pairs.append((src.at[at], dst.at[at]))
        return [pltpu.make_async_copy(a, b, sem.at[g, n]) for n, (a, b) in enumerate(pairs)]

    def arrive(g):
        for copy in chunk(g):
            copy.wait()

    def scale(x):
        for j in both:
            scaled = time_step * vh[x, :, LANES[j]] / vcap[x, :, LANES[j]]
            st[j, 0, x + 1, TOP : TOP + rows, :] = scaled

    if fresh:
        for g in range(nx // STEP):
            for copy in chunk(g):
                copy.start()
        for c in range(chans):
            clear_rim(st, nx, rows, c)
        clear_rim(kc, nx, rows)

        def rims(x, carry):
            rim = jnp.zeros((1, 128), F32)
            for j in both:
                for at in (slice(TOP - 1, TOP), slice(TOP + rows, TOP + rows + 1)):
                    for c in range(chans):
                        st[j, c, x, at, :] = rim
                    kc[j, x, at, :] = rim
            return carry

        lax.fori_loop(1, nx + 1, rims, 0)
        arrive(0)
        scale(0)
        scale(1)

    def plane(x, carry):
        if fresh:

            @pl.when((x % STEP == STEP - 2) & (x < nx - 2))
            def _():
                arrive(x // STEP + 1)

        for r in range(0, rows, RB):
            at = TOP + r
            body = slice(r, r + RB)

            def sides(ref, *lead):
                near = [
                    [
                        ref[(j, *lead, x, slice(at, at + RB))],
                        ref[(j, *lead, x + 2, slice(at, at + RB))],
                        ref[(j, *lead, x + 1, slice(at - 1, at - 1 + RB))],
                        ref[(j, *lead, x + 1, slice(at + 1, at + 1 + RB))],
                    ]
                    for j in both
                ]
                return [ref[(j, *lead, x + 1, slice(at, at + RB))] for j in both], near

            rt = [time_step * rate[x, body, LANES[j]] for j in both]
            if fresh:
                mt = [mat[x, body, LANES[j]] for j in both]
                odd = [v % 2 == 1 for v in mt]
                high = [v >= 2 for v in mt]

            c_mid, c_near = sides(kc)
            s_mid, s_near = sides(st, 0)
            c_up, c_down = updown(c_mid)
            s_up, s_down = updown(s_mid)
            flow = []
            for j in both:
                acc = None
                near_c = c_near[j] + [c_up[j], c_down[j]]
                near_s = s_near[j] + [s_up[j], s_down[j]]
                for oc, os in zip(near_c, near_s):
                    term = (c_mid[j] + oc) * (os - s_mid[j])
                    acc = term if acc is None else acc + term
                flow.append(0.5 * acc)
            mids = []
            outs = [[None] * chans for _ in both]
            for c in range(nsp):
                mid, near = sides(st, c + 1)
                up, down = updown(mid)
                kd = time_step * diffusion[c]
                mids.append(mid)
                for j in both:
                    n4 = (near[j][0] + near[j][1]) + (near[j][2] + near[j][3])
                    n6 = n4 + (up[j] + down[j])
                    outs[j][c + 1] = mid[j] + kd * (n6 - 6.0 * mid[j])
            for j in both:
                source = None
                for c in range(nsp):
                    term = coupling[c] * mids[c][j]
                    source = term if source is None else source + term
                head = vh[x, body, LANES[j]] if fresh else h[j, x, body]
                out[j, 0, x, body, :] = head + flow[j] + rt[j] * source
            for s in range(nsp):
                acc = [outs[j][s + 1] for j in both]
                for t in range(nsp):
                    n = s * nsp + t
                    for j in both:
                        if fresh:
                            r0, r1, r2, r3 = (react[i, t, s] for i in range(4))
                            w = jnp.where(
                                high[j], jnp.where(odd[j], r3, r2), jnp.where(odd[j], r1, r0)
                            )
                            w = w * -rt[j]
                            coef[j, n, x, body, :] = w
                        else:
                            w = coef[j, n, x, body, :]
                        acc[j] = acc[j] + w * mids[t][j]
                for j in both:
                    out[j, s + 1, x, body, :] = acc[j]
        if fresh:
            scale(jnp.minimum(x + 2, nx - 1))
        return carry

    lax.fori_loop(0, nx, plane, 0)


def inner(diffusion, coupling, react, rate, h, coef, kc, st):
    nx, rows, _ = rate.shape
    chans = st.shape[1]
    return pl.pallas_call(
        functools.partial(inner_kernel, False, nx, rows, chans),
        in_specs=[SM] * 3 + [VM] * 5,
        out_specs=VM,
        out_shape=jax.ShapeDtypeStruct((2, chans, nx, rows, 128), F32),
        compiler_params=pltpu.CompilerParams(vmem_limit_bytes=2 * 2**20),
        cost_estimate=pl.CostEstimate(flops=6 * 10**7, bytes_accessed=3 * 10**7, transcendentals=0),
    )(diffusion, coupling, react, rate, h, coef, kc, st)


def first_inner(diffusion, coupling, react, rate, h, mat, cap, sp, cond):
    nx, rows, depth = rate.shape
    nsp = sp.shape[0]
    chans = nsp + 1
    shape = lambda *dims: jax.ShapeDtypeStruct(dims, F32)
    padded = (nx + 2, rows + 2 * TOP, 128)
    return pl.pallas_call(
        functools.partial(inner_kernel, True, nx, rows, chans),
        in_specs=[SM] * 3 + [VM, HB, VM, HB, HB, HB],
        out_specs=[VM] * 3,
        out_shape=[
            shape(2, nsp * nsp, nx, rows, 128),
            shape(2, *padded),
            shape(2, chans, nx, rows, 128),
        ],
        scratch_shapes=[
            pltpu.VMEM((2, chans, *padded), F32),
            pltpu.VMEM((nx, rows, depth), F32),
            pltpu.VMEM((nx, rows, depth), F32),
            pltpu.SemaphoreType.DMA((nx // STEP, 6)),
        ],
        compiler_params=pltpu.CompilerParams(vmem_limit_bytes=12 * 2**20),
        cost_estimate=pl.CostEstimate(flops=6 * 10**7, bytes_accessed=3 * 10**7, transcendentals=0),
    )(diffusion, coupling, react, rate, h, mat, cap, sp, cond)


def close_kernel(k, last, nx, rows, chans, *refs):
    refs = list(refs)
    take = lambda n: [refs.pop(0) for _ in range(n)]
    (diffusion,) = take(1)
    sums = take(k + 1)
    hot, inn, kc, cap, mask = take(5)
    ox1, ox2, oya, oyb = take(4)
    xr1, xr2, ya, yb = take(4)
    cx1, cx2, cya, cyb = (xr1, xr2, ya, yb) if k == 0 else take(4)
    if last:
        oh, osp = take(2)
    else:
        oh, ost, px1, px2, pa, pb = take(6)
    ansb, half, xh = take(3)
    if last:
        th, tsp, sem = take(3)

    n_pipes = 256
    nsp = chans - 1
    even_x, even_y, gy = edge_flags()
    last_y = lax.axis_size("gy") - 1

    t0 = sums[0]
    root = jnp.sqrt(t0[0, 7:8, :] + 1.0)
    observed = t0[1]
    row = lax.broadcasted_iota(jnp.int32, (8, n_pipes), 0)
    answer = jnp.tanh(observed - t0[0] / root)
    if k > 0:
        weight = drain_gain * jnp.where(row == 0, sums[1][0, 7:8, :], t0[0, 7:8, :])
    for later in sums[1:]:
        answer = jnp.tanh(observed - (later[0] + answer * weight) / root)
    answer = drain_gain * answer
    tall = jnp.transpose(jnp.concatenate([answer, jnp.zeros((120, n_pipes), F32)], axis=0))
    pieces = jnp.concatenate(split(tall, 2), axis=1)
    part_of = lax.broadcasted_iota(jnp.int32, (256, 256), 1) // 128
    chan_of = lax.broadcasted_iota(jnp.int32, (256, 256), 0) % 128
    for j in range(2):
        picked = jnp.dot(hot[j], pieces, preferred_element_type=F32).astype(BF16)
        for c in range(0, chans, 2):
            spread = (part_of + c == chan_of).astype(BF16)
            wide = jnp.dot(picked, spread, preferred_element_type=F32)
            ansb[j, c] = wide[:, :128]
            if c + 1 < chans:
                ansb[j, c + 1] = wide[:, 128:]

    a_lo = jnp.where(even_y, 0.0, 1.0)
    b_lo = jnp.where(even_y & (gy > 0), 1.0, 0.0)
    a_hi = jnp.where(even_y, 1.0, 0.0)
    b_hi = jnp.where(even_y | (gy == last_y), 0.0, 1.0)
    row = lax.broadcasted_iota(jnp.int32, (8, 128), 0)
    top, bottom = row == 0, row == 7
    gains = jnp.zeros((8, 128), F32)
    for c in range(nsp):
        gains = jnp.where(row == c + 1, time_step * diffusion[c], gains)
    rim = jnp.zeros((TOP, 128), F32)
    if not last:
        for c in range(chans):
            clear_rim(ost, nx, rows, c)

    def pull(c_mid, s_mid, c_far, s_far):
        return 0.5 * ((c_mid + c_far) * s_far - c_far * s_mid)

    def keep(n, near, cnear, own):
        xh[n, chans + 1] = own[0]
        for c in range(chans):
            xh[n, c] = near[c]
        xh[n, chans] = cnear[chans]

    @pl.when(even_x)
    def _():
        keep(0, xr2, cx2, ox2)
        keep(1, xr1, cx1, ox1)

    @pl.when(jnp.logical_not(even_x))
    def _():
        keep(0, xr1, cx1, ox1)
        keep(1, xr2, cx2, ox2)

    def work(x, rim_at):
        for j, part in enumerate(LANES):
            def rims_of(ra, rb, wa, wb):
                return ra[x, :, part] * wa + rb[x, :, part] * wb

            m = mask[x, :, part].astype(F32)
            c_all = kc[j, x + 1, TOP : TOP + rows, :]
            add = []
            for at, wa, wb in ((0, a_lo, b_lo), (rows - 1, a_hi, b_hi)):
                far = rims_of(ya, yb, wa, wb)
                c_far = far if k == 0 else rims_of(cya, cyb, wa, wb)
                c_far = c_far[chans : chans + 1]
                s_mid = jnp.where(even_y == (at > 0), oya[x, 0:1, part], oyb[x, 0:1, part])
                head = pull(kc[j, x + 1, TOP + at : TOP + at + 1, :], s_mid, c_far, far[0:1])
                add.append((head, gains * far))
            values = []
            for c in range(chans):
                v = inn[j, c, x]
                lo, hi = ((a[0] if c == 0 else a[1][c : c + 1]) for a in add)
                v = jnp.concatenate(
                    [
                        v[:8] + jnp.where(top, lo, 0.0),
                        v[8 : rows - 8],
                        v[rows - 8 :] + jnp.where(bottom, hi, 0.0),
                    ],
                    axis=0,
                )
                if rim_at is not None:
                    far = xh[rim_at, c, :, part]
                    if c == 0:
                        v = v + pull(c_all, xh[rim_at, chans + 1, :, part], xh[rim_at, chans, :, part], far)
                    else:
                        v = v + time_step * diffusion[c - 1] * far
                values.append(v)
            if not last:
                drained = [v * m for v in values]
                drained[0] = drained[0] * c_all
                drained.append(c_all * m)
                for c, v in enumerate(halve(drained)):
                    half[j, c, pl.ds(x * rows, rows), :] = v
            for c, v in enumerate(values):
                v = v + m * ansb[j, c, pl.ds(x * rows, rows), :]
                if last:
                    if c == 0:
                        th[x, :, part] = v
                    else:
                        tsp[c - 1, x, :, part] = v
                    continue
                if c == 0:
                    oh[j, x] = v
                    v = time_step * v / cap[x, :, part]
                ost[j, c, x + 1, TOP : TOP + rows, :] = v
                ost[j, c, x + 1, 0:TOP, :] = rim
                ost[j, c, x + 1, TOP + rows : 2 * TOP + rows, :] = rim
                lo, hi = v[0:1], v[rows - 1 : rows]
                pa[x, c : c + 1, part] = jnp.where(even_y, hi, lo)
                pb[x, c : c + 1, part] = jnp.where(even_y, lo, hi)

    def result(g):
        at = pl.ds(g * STEP, STEP)
        pairs = [(th.at[at], oh.at[at]), (tsp.at[:, at], osp.at[:, at])]
        return [pltpu.make_async_copy(a, b, sem.at[g, n]) for n, (a, b) in enumerate(pairs)]

    def planes(i, carry):
        x = 2 * i
        work(x - 1, None)
        if last:

            @pl.when(x % STEP == 0)
            def _():
                for copy in result(x // STEP - 1):
                    copy.start()

        work(x, None)
        return carry

    work(0, 0)
    work(nx - 1, 1)
    lax.fori_loop(1, nx // 2, planes, 0)
    if not last:

        def send(dst, x):
            for c in range(chans):
                for j, part in enumerate(LANES):
                    dst[c, :, part] = ost[j, c, x + 1, TOP : TOP + rows, :]

        @pl.when(even_x)
        def _():
            send(px1, nx - 1)
            send(px2, 0)

        @pl.when(jnp.logical_not(even_x))
        def _():
            send(px1, 0)
            send(px2, nx - 1)

        total = pipe_sums(half, hot)
        pa[nx] = total
        pb[nx] = total
    else:
        for copy in result(nx // STEP - 1):
            copy.start()
        for g in range(nx // STEP):
            for copy in result(g):
                copy.wait()


def close(k, diffusion, sums, hot, inn, kc, cap, mask, own, near, near0):
    last = k == ITERS - 1
    nx, rows, depth = cap.shape
    chans = inn.shape[1]
    n_pipes = 256
    args = [diffusion, *sums, hot, inn, kc, cap, mask, *own, *near]
    if k > 0:
        args += near0
    shape = lambda *dims: jax.ShapeDtypeStruct(dims, F32)
    scratch = [
        pltpu.VMEM((2, chans, nx * rows, 128), F32),
        pltpu.VMEM((2, 4, nx * rows, 128), F32),
        pltpu.VMEM((2, chans + 2, rows, depth), F32),
    ]
    if last:
        shapes = [shape(nx, rows, depth), shape(chans - 1, nx, rows, depth)]
        out_specs = [HB] * 2
        scratch += [
            pltpu.VMEM((nx, rows, depth), F32),
            pltpu.VMEM((chans - 1, nx, rows, depth), F32),
            pltpu.SemaphoreType.DMA((nx // STEP, 2)),
        ]
    else:
        shapes = [shape(2, nx, rows, 128), shape(2, chans, nx + 2, rows + 2 * TOP, 128)]
        shapes += [shape(chans, rows, depth)] * 2 + [shape(nx + 1, 8, n_pipes)] * 2
        out_specs = [VM] * 6
    return pl.pallas_call(
        functools.partial(close_kernel, k, last, nx, rows, chans),
        in_specs=[SM] + [VM] * (len(args) - 1),
        out_specs=out_specs,
        out_shape=shapes,
        scratch_shapes=scratch,
        compiler_params=pltpu.CompilerParams(vmem_limit_bytes=VLIM),
        cost_estimate=pl.CostEstimate(flops=2 * 10**7, bytes_accessed=10**7, transcendentals=0),
    )(*args)


def swap(x, axis, first_low):
    count = lax.axis_size(axis)
    pairs = []
    for low in range(first_low, count - 1, 2):
        pairs += [(low, low + 1), (low + 1, low)]
    return lax.ppermute(x, axis, pairs)


def beside_x(px1, px2):
    return [swap(px1, "gx", 0), swap(px2, "gx", 1)]


def beside_y(pa, pb, nx):
    count = lax.axis_size("gy")
    ya = swap(pa, "gy", 0)
    pair_sum = pa[nx:] + ya[nx:]
    pb = lax.dynamic_update_slice(pb, pair_sum, (nx, 0, 0))
    ring = []
    for low in range(1, count, 2):
        other = (low + 1) % count
        ring += [(low, other), (other, low)]
    yb = lax.ppermute(pb, "gy", ring)
    four = pair_sum + yb[nx:]
    far = lax.ppermute(four, "gy", [(i, (i + count // 2) % count) for i in range(count)])
    return [ya, yb], four + far


def body(
    adj_head,
    adj_species,
    cond,
    capacity,
    rate,
    diffusion,
    coupling,
    react,
    material,
    drain_mask,
    block_pipe,
    pipe_obs,
):
    nx = adj_head.shape[0]
    pipes = jnp.transpose(block_pipe, (0, 2, 1))
    *packs, pa, pb, hot = first(
        adj_head, adj_species, cond, capacity, drain_mask, pipes, pipe_obs
    )
    near_x = beside_x(*packs)
    near0 = None
    sums = []
    for k in range(ITERS):
        near_y, total = beside_y(pa, pb, nx)
        near = near_x + near_y
        near0 = near if k == 0 else near0
        sums.append(total)
        if k == 0:
            coef, kc, inn = first_inner(
                diffusion, coupling, react, rate, adj_head, material, capacity, adj_species, cond
            )
        else:
            inn = inner(diffusion, coupling, react, rate, h, coef, kc, st)
        own = [*packs, pa, pb]
        out = close(k, diffusion, sums, hot, inn, kc, capacity, drain_mask, own, near, near0)
        if k < ITERS - 1:
            h, st, *packs, pa, pb = out
            near_x = beside_x(*packs)
    return tuple(out)


def solution(mesh):
    return jax.shard_map(
        body,
        mesh=mesh,
        in_specs=(
            P("gx", "gy", None),
            P(None, "gx", "gy", None),
            P("gx", "gy", None),
            P("gx", "gy", None),
            P("gx", "gy", None),
            P(),
            P(),
            P(),
            P("gx", "gy", None),
            P("gx", "gy", None),
            P("gx", "gy", None),
            P(None, "gx", "gy"),
        ),
        out_specs=(P("gx", "gy", None), P(None, "gx", "gy", None)),
        check_vma=False,
    )
```

```python
import functools

import jax
import jax.numpy as jnp
from jax import lax
from jax.experimental import pallas as pl
from jax.experimental.pallas import tpu as pltpu
from jax.sharding import PartitionSpec as P

ITERS = 3
time_step = 0.08
drain_gain = 0.5

F32 = jnp.float32
BF16 = jnp.bfloat16
HB = pl.BlockSpec(memory_space=pltpu.HBM)
ANY = pl.BlockSpec(memory_space=pl.ANY)
VM = pl.BlockSpec(memory_space=pltpu.VMEM)
SM = pl.BlockSpec(memory_space=pltpu.SMEM)
TOP = 8
STEP = 4
RB = 16


VLIM = 14 * 2**20
LANES = (slice(0, 128), slice(128, 256))


def split(x, pieces):
    out = []
    for _ in range(pieces):
        piece = x.astype(BF16)
        out.append(piece)
        x = x - piece.astype(F32)
    return out


def block_onehots(bp, hot):
    nx, blocks, rows = bp.shape
    n_pipes = hot.shape[2]
    flat = bp[...].astype(F32).reshape(nx * blocks, rows)
    flat = jnp.concatenate([flat, jnp.zeros((128 - nx * blocks, rows), F32)], axis=0)
    tall = jnp.transpose(jnp.concatenate([flat, jnp.zeros((128, 128 - rows), F32)], axis=1))
    pipe = lax.broadcasted_iota(jnp.int32, (rows, n_pipes), 1).astype(F32)
    for x in range(nx):
        for j in range(blocks):
            n = x * blocks + j
            match = tall[:rows, n : n + 1] == pipe
            hot[j, x * rows : (x + 1) * rows, :] = match.astype(BF16)


def turn(x, by):
    return pltpu.roll(x, (-by) % 128, 1)


def halve(values):
    low = lax.broadcasted_iota(jnp.int32, values[0].shape, 1) < 64
    return [
        jnp.where(low, a, b) + turn(jnp.where(low, b, a), 64)
        for a, b in zip(values[::2], values[1::2])
    ]


def merge(level):
    lane = lax.broadcasted_iota(jnp.int32, level[0].shape, 1)
    for width in (32, 16):
        low = lane & width == 0
        level = [
            jnp.where(low, a, b) + jnp.where(low, turn(a, width), turn(b, -width))
            for a, b in zip(level[::2], level[1::2])
        ]
    return level[0]


SUM_LANE = [64 * (c & 1) + 32 * (c >> 1 & 1) + 16 * (c >> 2 & 1) for c in range(8)]
CHUNK = 128


def block_sums(half, j):
    lane = lax.broadcasted_iota(jnp.int32, (16, 128), 1) // 16
    chan = lax.broadcasted_iota(jnp.int32, (16, 128), 0)
    group = 4 * (chan & 1) + 2 * (chan >> 1 & 1) + (chan >> 2 & 1)
    pick = ((lane == group) & (chan < 8)).astype(BF16)
    out = []
    for r in range(0, half.shape[2], CHUNK):
        merged = merge([half[j, c, r : r + CHUNK, :] for c in range(4)])
        total = None
        for piece in split(merged, 3)[::-1]:
            part = lax.dot_general(
                pick, piece, (((1,), (1,)), ((), ())), preferred_element_type=F32
            )
            total = part if total is None else total + part
        out.append(total)
    return jnp.concatenate(out, axis=1)[:8]


def pipe_sums(half, hot):
    total = None
    for j in range(2):
        rows = block_sums(half, j)
        stack = jnp.concatenate(split(rows, 3) + [jnp.zeros(rows.shape, BF16)], axis=0)
        part = jnp.dot(stack, hot[j], preferred_element_type=F32)
        total = part if total is None else total + part
    return (total[16:24] + total[8:16]) + total[:8]


def edge_flags():
    gx, gy = lax.axis_index("gx"), lax.axis_index("gy")
    return gx % 2 == 0, gy % 2 == 0, gy


def clear_rim(ref, nx, rows, *lead):
    tile = jnp.zeros((TOP, 128), F32)
    for j in range(2):
        for x in (0, nx + 1):
            for r in range(0, rows + 2 * TOP, TOP):
                ref[(j, *lead, x, slice(r, r + TOP))] = tile


def first_kernel(
    nx, rows, chans, h, sp, cond, cap, mask, bp, obs, px1, px2, pa, pb, hot,
    half, vh, vs, vk, vcap, vmask, sem, tiny_sem, vbp, vobs
):
    even_x, even_y, gy = edge_flags()
    n_pipes = pa.shape[2]

    def chunk(g):
        at = pl.ds(g * STEP, STEP)
        pairs = [(sp.at[:, at], vs.at[:, at])]
        for src, dst in ((h, vh), (cond, vk), (cap, vcap), (mask, vmask)):
            pairs.append((src.at[at], dst.at[at]))
        return [pltpu.make_async_copy(a, b, sem.at[g, n]) for n, (a, b) in enumerate(pairs)]

    tiny = [pltpu.make_async_copy(bp, vbp, tiny_sem.at[0]), pltpu.make_async_copy(obs, vobs, tiny_sem.at[1])]
    for copy in tiny:
        copy.start()
    for g in range(nx // STEP):
        for copy in chunk(g):
            copy.start()
    for copy in tiny:
        copy.wait()
    block_onehots(vbp, hot)

    def planes(i, carry):
        @pl.when(i % (STEP // 2) == 0)
        def _():
            for copy in chunk(i // (STEP // 2)):
                copy.wait()

        work(2 * i)
        work(2 * i + 1)
        return carry

    def work(x):
        for j, part in enumerate(LANES):
            cd = vk[x, :, part]
            head = vh[x, :, part]
            m = vmask[x, :, part].astype(F32)
            scaled = time_step * head / vcap[x, :, part]
            species = [vs[c, x, :, part] for c in range(chans - 1)]
            for c, field in enumerate([scaled, *species, cd]):
                lo, hi = field[0:1], field[rows - 1 : rows]
                pa[x, c : c + 1, part] = jnp.where(even_y, hi, lo)
                pb[x, c : c + 1, part] = jnp.where(even_y, lo, hi)
            sums = halve([cd * m * head] + [v * m for v in species] + [m])
            place = pl.ds(x * rows, rows)
            for c in range(4):
                half[j, c, place, :] = sums[c]

    lax.fori_loop(0, nx // 2, planes, 0)

    def send(dst, x):
        dst[0] = time_step * vh[x] / vcap[x]
        for c in range(chans - 1):
            dst[c + 1] = vs[c, x]
        dst[chans] = vk[x]

    @pl.when(even_x)
    def _():
        send(px1, nx - 1)
        send(px2, 0)

    @pl.when(jnp.logical_not(even_x))
    def _():
        send(px1, 0)
        send(px2, nx - 1)

    total = pipe_sums(half, hot)
    small = vobs[:, 0, :]
    wide = jnp.concatenate([small] * (n_pipes // small.shape[1]), axis=1)
    place = lax.broadcasted_iota(jnp.int32, wide.shape, 1) // small.shape[1]
    mine = jnp.where(place == gy, wide, 0.0)
    second = jnp.concatenate([mine, jnp.zeros((1, n_pipes), F32)], axis=0)
    for dst in (pa, pb):
        dst[nx] = total
        dst[nx + 1] = second


def first(h, sp, cond, cap, mask, bp, obs):
    nx, rows, depth = h.shape
    chans = sp.shape[0] + 1
    n_pipes = 256
    shape = lambda *dims: jax.ShapeDtypeStruct(dims, F32)
    field = lambda dtype: pltpu.VMEM((nx, rows, depth), dtype)
    return pl.pallas_call(
        functools.partial(first_kernel, nx, rows, chans),
        in_specs=[HB] * 7,
        out_specs=[VM] * 5,
        out_shape=[
            shape(chans + 1, rows, depth),
            shape(chans + 1, rows, depth),
            shape(nx + 2, 8, n_pipes),
            shape(nx + 2, 8, n_pipes),
            jax.ShapeDtypeStruct((2, nx * rows, n_pipes), BF16),
        ],
        scratch_shapes=[
            pltpu.VMEM((2, 4, nx * rows, 128), F32),
            field(F32),
            pltpu.VMEM(sp.shape, F32),
            field(F32),
            field(F32),
            field(jnp.int32),
            pltpu.SemaphoreType.DMA((nx // STEP, 5)),
            pltpu.SemaphoreType.DMA((2,)),
            pltpu.VMEM(bp.shape, jnp.int32),
            pltpu.VMEM(obs.shape, F32),
        ],
        compiler_params=pltpu.CompilerParams(vmem_limit_bytes=53 * 2**20),
        cost_estimate=pl.CostEstimate(flops=10**7, bytes_accessed=8 * 10**6, transcendentals=0),
    )(h, sp, cond, cap, mask, bp, obs)


def inner_kernel(fresh, nx, rows, chans, diffusion, coupling, *refs):
    if fresh:
        react, rate, h, mat, cap, sp, cond, coef, kc, out, st, vh, vcap, sem = refs
    else:
        rate, h, coef, kc, st, out = refs
    nsp = chans - 1
    both = range(2)
    gains = diffusion[...].reshape(1, nsp)
    heads = coupling[...].reshape(1, nsp)
    diffusion = [jnp.broadcast_to(gains[:, c : c + 1], (RB, 128)) for c in range(nsp)]
    coupling = [jnp.broadcast_to(heads[:, c : c + 1], (RB, 128)) for c in range(nsp)]
    lane = lax.broadcasted_iota(jnp.int32, (RB, 128), 1)
    first_lane, last_lane = lane == 0, lane == 127

    def updown(pair):
        left = [turn(v, -1) for v in pair]
        right = [turn(v, 1) for v in pair]
        up = [jnp.where(first_lane, 0.0, left[0]), jnp.where(first_lane, left[0], left[1])]
        down = [jnp.where(last_lane, right[1], right[0]), jnp.where(last_lane, 0.0, right[1])]
        return up, down

    def chunk(g):
        at, into = pl.ds(g * STEP, STEP), pl.ds(g * STEP + 1, STEP)
        inside = pl.ds(TOP, rows)
        pairs = []
        for j, part in enumerate((pl.ds(0, 128), pl.ds(128, 128))):
            pairs.append((sp.at[:, at, :, part], st.at[j, pl.ds(1, nsp), into, inside, :]))
            pairs.append((cond.at[at, :, part], kc.at[j, into, inside, :]))
        for src, dst in ((h, vh), (cap, vcap)):
            pairs.append((src.at[at], dst.at[at]))
        return [pltpu.make_async_copy(a, b, sem.at[g, n]) for n, (a, b) in enumerate(pairs)]

    def arrive(g):
        for copy in chunk(g):
            copy.wait()

    def scale(x):
        for j in both:
            scaled = time_step * vh[x, :, LANES[j]] / vcap[x, :, LANES[j]]
            st[j, 0, x + 1, TOP : TOP + rows, :] = scaled

    if fresh:
        for g in range(nx // STEP):
            for copy in chunk(g):
                copy.start()
        for c in range(chans):
            clear_rim(st, nx, rows, c)
        clear_rim(kc, nx, rows)

        def rims(x, carry):
            rim = jnp.zeros((1, 128), F32)
            for j in both:
                for at in (slice(TOP - 1, TOP), slice(TOP + rows, TOP + rows + 1)):
                    for c in range(chans):
                        st[j, c, x, at, :] = rim
                    kc[j, x, at, :] = rim
            return carry

        lax.fori_loop(1, nx + 1, rims, 0)
        arrive(0)
        scale(0)
        scale(1)
        scale(2)

    def planes(i, carry):
        x = 2 * i
        if fresh:

            @pl.when((x % STEP == 0) & (x < nx - STEP))
            def _():
                arrive(x // STEP + 1)

        plane(x)
        plane(x + 1)
        if fresh:
            scale(jnp.minimum(x + 3, nx - 1))
            scale(jnp.minimum(x + 4, nx - 1))
        return carry

    def plane(x):
        for r in range(0, rows, RB):
            at = TOP + r
            body = slice(r, r + RB)

            def sides(ref, *lead):
                near = [
                    [
                        ref[(j, *lead, x, slice(at, at + RB))],
                        ref[(j, *lead, x + 2, slice(at, at + RB))],
                        ref[(j, *lead, x + 1, slice(at - 1, at - 1 + RB))],
                        ref[(j, *lead, x + 1, slice(at + 1, at + 1 + RB))],
                    ]
                    for j in both
                ]
                return [ref[(j, *lead, x + 1, slice(at, at + RB))] for j in both], near

            rt = [time_step * rate[x, body, LANES[j]] for j in both]
            if fresh:
                mt = [mat[x, body, LANES[j]] for j in both]
                odd = [v % 2 == 1 for v in mt]
                high = [v >= 2 for v in mt]

            c_mid, c_near = sides(kc)
            s_mid, s_near = sides(st, 0)
            c_up, c_down = updown(c_mid)
            s_up, s_down = updown(s_mid)
            flow = []
            for j in both:
                acc = None
                near_c = c_near[j] + [c_up[j], c_down[j]]
                near_s = s_near[j] + [s_up[j], s_down[j]]
                for oc, os in zip(near_c, near_s):
                    term = (c_mid[j] + oc) * (os - s_mid[j])
                    acc = term if acc is None else acc + term
                flow.append(0.5 * acc)
            mids = []
            outs = [[None] * chans for _ in both]
            for c in range(nsp):
                mid, near = sides(st, c + 1)
                up, down = updown(mid)
                kd = time_step * diffusion[c]
                mids.append(mid)
                for j in both:
                    n4 = (near[j][0] + near[j][1]) + (near[j][2] + near[j][3])
                    n6 = n4 + (up[j] + down[j])
                    outs[j][c + 1] = mid[j] + kd * (n6 - 6.0 * mid[j])
            for j in both:
                source = None
                for c in range(nsp):
                    term = coupling[c] * mids[c][j]
                    source = term if source is None else source + term
                head = vh[x, body, LANES[j]] if fresh else h[j, x, body]
                out[j, 0, x, body, :] = head + flow[j] + rt[j] * source
            for s in range(nsp):
                acc = [outs[j][s + 1] for j in both]
                for t in range(nsp):
                    n = s * nsp + t
                    for j in both:
                        if fresh:
                            r0, r1, r2, r3 = (react[i, t, s] for i in range(4))
                            w = jnp.where(
                                high[j], jnp.where(odd[j], r3, r2), jnp.where(odd[j], r1, r0)
                            )
                            w = w * -rt[j]
                            coef[j, n, x, body, :] = w
                        else:
                            w = coef[j, n, x, body, :]
                        acc[j] = acc[j] + w * mids[t][j]
                for j in both:
                    out[j, s + 1, x, body, :] = acc[j]

    lax.fori_loop(0, nx // 2, planes, 0)


def inner(diffusion, coupling, react, rate, h, coef, kc, st):
    nx, rows, _ = rate.shape
    chans = st.shape[1]
    return pl.pallas_call(
        functools.partial(inner_kernel, False, nx, rows, chans),
        in_specs=[VM] * 2 + [VM] * 5,
        out_specs=VM,
        out_shape=jax.ShapeDtypeStruct((2, chans, nx, rows, 128), F32),
        compiler_params=pltpu.CompilerParams(vmem_limit_bytes=2 * 2**20),
        cost_estimate=pl.CostEstimate(flops=6 * 10**7, bytes_accessed=3 * 10**7, transcendentals=0),
    )(diffusion, coupling, rate, h, coef, kc, st)


def first_inner(diffusion, coupling, react, rate, h, mat, cap, sp, cond):
    nx, rows, depth = rate.shape
    nsp = sp.shape[0]
    chans = nsp + 1
    shape = lambda *dims: jax.ShapeDtypeStruct(dims, F32)
    padded = (nx + 2, rows + 2 * TOP, 128)
    return pl.pallas_call(
        functools.partial(inner_kernel, True, nx, rows, chans),
        in_specs=[VM, VM, SM, VM, HB, VM, HB, HB, HB],
        out_specs=[VM] * 3,
        out_shape=[
            shape(2, nsp * nsp, nx, rows, 128),
            shape(2, *padded),
            shape(2, chans, nx, rows, 128),
        ],
        scratch_shapes=[
            pltpu.VMEM((2, chans, *padded), F32),
            pltpu.VMEM((nx, rows, depth), F32),
            pltpu.VMEM((nx, rows, depth), F32),
            pltpu.SemaphoreType.DMA((nx // STEP, 6)),
        ],
        compiler_params=pltpu.CompilerParams(vmem_limit_bytes=12 * 2**20),
        cost_estimate=pl.CostEstimate(flops=6 * 10**7, bytes_accessed=3 * 10**7, transcendentals=0),
    )(diffusion, coupling, react, rate, h, mat, cap, sp, cond)


def close_kernel(k, last, nx, rows, chans, *refs):
    refs = list(refs)
    take = lambda n: [refs.pop(0) for _ in range(n)]
    (diffusion,) = take(1)
    sums = take(k + 1)
    hot, inn, kc, cap, mask = take(5)
    ox1, ox2, oya, oyb = take(4)
    xr1, xr2, ya, yb = take(4)
    cx1, cx2, cya, cyb = (xr1, xr2, ya, yb) if k == 0 else take(4)
    if last:
        oh, osp = take(2)
    else:
        oh, ost, px1, px2, pa, pb = take(6)
    ansb, half, xh = take(3)
    if last:
        th, tsp, sem = take(3)

    n_pipes = 256
    nsp = chans - 1
    even_x, even_y, gy = edge_flags()
    last_y = lax.axis_size("gy") - 1

    t0 = sums[0]
    root = jnp.sqrt(t0[0, 7:8, :] + 1.0)
    observed = t0[1]
    row = lax.broadcasted_iota(jnp.int32, (8, n_pipes), 0)
    answer = jnp.tanh(observed - t0[0] / root)
    if k > 0:
        weight = drain_gain * jnp.where(row == 0, sums[1][0, 7:8, :], t0[0, 7:8, :])
    for later in sums[1:]:
        answer = jnp.tanh(observed - (later[0] + answer * weight) / root)
    answer = drain_gain * answer
    tall = jnp.transpose(jnp.concatenate([answer, jnp.zeros((120, n_pipes), F32)], axis=0))
    pieces = jnp.concatenate(split(tall, 2), axis=1)
    part_of = lax.broadcasted_iota(jnp.int32, (256, 256), 1) // 128
    chan_of = lax.broadcasted_iota(jnp.int32, (256, 256), 0) % 128
    for j in range(2):
        picked = jnp.dot(hot[j], pieces, preferred_element_type=F32).astype(BF16)
        for c in range(0, chans, 2):
            spread = (part_of + c == chan_of).astype(BF16)
            wide = jnp.dot(picked, spread, preferred_element_type=F32)
            ansb[j, c] = wide[:, :128]
            if c + 1 < chans:
                ansb[j, c + 1] = wide[:, 128:]

    a_lo = jnp.where(even_y, 0.0, 1.0)
    b_lo = jnp.where(even_y & (gy > 0), 1.0, 0.0)
    a_hi = jnp.where(even_y, 1.0, 0.0)
    b_hi = jnp.where(even_y | (gy == last_y), 0.0, 1.0)
    row = lax.broadcasted_iota(jnp.int32, (8, 128), 0)
    top, bottom = row == 0, row == 7
    gains = jnp.zeros((8, 128), F32)
    share = time_step * diffusion[...].reshape(1, nsp)
    shares = [share[:, c : c + 1] for c in range(nsp)]
    for c in range(nsp):
        gains = jnp.where(row == c + 1, shares[c], gains)
    rim = jnp.zeros((TOP, 128), F32)
    if not last:
        for c in range(chans):
            clear_rim(ost, nx, rows, c)

    def pull(c_mid, s_mid, c_far, s_far):
        return 0.5 * ((c_mid + c_far) * s_far - c_far * s_mid)

    def keep(n, near, cnear, own):
        xh[n, chans + 1] = own[0]
        for c in range(chans):
            xh[n, c] = near[c]
        xh[n, chans] = cnear[chans]

    @pl.when(even_x)
    def _():
        keep(0, xr2, cx2, ox2)
        keep(1, xr1, cx1, ox1)

    @pl.when(jnp.logical_not(even_x))
    def _():
        keep(0, xr1, cx1, ox1)
        keep(1, xr2, cx2, ox2)

    def work(x, rim_at):
        for j, part in enumerate(LANES):
            def rims_of(ra, rb, wa, wb):
                return ra[x, :, part] * wa + rb[x, :, part] * wb

            m = mask[x, :, part].astype(F32)
            c_all = kc[j, x + 1, TOP : TOP + rows, :]
            add = []
            for at, wa, wb in ((0, a_lo, b_lo), (rows - 1, a_hi, b_hi)):
                far = rims_of(ya, yb, wa, wb)
                c_far = far if k == 0 else rims_of(cya, cyb, wa, wb)
                c_far = c_far[chans : chans + 1]
                s_mid = jnp.where(even_y == (at > 0), oya[x, 0:1, part], oyb[x, 0:1, part])
                head = pull(kc[j, x + 1, TOP + at : TOP + at + 1, :], s_mid, c_far, far[0:1])
                add.append((head, gains * far))
            values = []
            for c in range(chans):
                v = inn[j, c, x]
                lo, hi = ((a[0] if c == 0 else a[1][c : c + 1]) for a in add)
                v = jnp.concatenate(
                    [
                        v[:8] + jnp.where(top, lo, 0.0),
                        v[8 : rows - 8],
                        v[rows - 8 :] + jnp.where(bottom, hi, 0.0),
                    ],
                    axis=0,
                )
                if rim_at is not None:
                    far = xh[rim_at, c, :, part]
                    if c == 0:
                        v = v + pull(c_all, xh[rim_at, chans + 1, :, part], xh[rim_at, chans, :, part], far)
                    else:
                        v = v + shares[c - 1] * far
                values.append(v)
            if not last:
                drained = [v * m for v in values]
                drained[0] = drained[0] * c_all
                drained.append(c_all * m)
                for c, v in enumerate(halve(drained)):
                    half[j, c, pl.ds(x * rows, rows), :] = v
            for c, v in enumerate(values):
                v = v + m * ansb[j, c, pl.ds(x * rows, rows), :]
                if last:
                    if c == 0:
                        th[x, :, part] = v
                    else:
                        tsp[c - 1, x, :, part] = v
                    continue
                if c == 0:
                    oh[j, x] = v
                    v = time_step * v / cap[x, :, part]
                ost[j, c, x + 1, TOP : TOP + rows, :] = v
                ost[j, c, x + 1, 0:TOP, :] = rim
                ost[j, c, x + 1, TOP + rows : 2 * TOP + rows, :] = rim
                lo, hi = v[0:1], v[rows - 1 : rows]
                pa[x, c : c + 1, part] = jnp.where(even_y, hi, lo)
                pb[x, c : c + 1, part] = jnp.where(even_y, lo, hi)

    def result(g):
        at = pl.ds(g * STEP, STEP)
        pairs = [(th.at[at], oh.at[at]), (tsp.at[:, at], osp.at[:, at])]
        return [pltpu.make_async_copy(a, b, sem.at[g, n]) for n, (a, b) in enumerate(pairs)]

    def planes(i, carry):
        x = 2 * i
        work(x - 1, None)
        if last:

            @pl.when(x % STEP == 0)
            def _():
                for copy in result(x // STEP - 1):
                    copy.start()

        work(x, None)
        return carry

    work(0, 0)
    work(nx - 1, 1)
    lax.fori_loop(1, nx // 2, planes, 0)
    if not last:

        def send(dst, x):
            for c in range(chans):
                for j, part in enumerate(LANES):
                    dst[c, :, part] = ost[j, c, x + 1, TOP : TOP + rows, :]

        @pl.when(even_x)
        def _():
            send(px1, nx - 1)
            send(px2, 0)

        @pl.when(jnp.logical_not(even_x))
        def _():
            send(px1, 0)
            send(px2, nx - 1)

        total = pipe_sums(half, hot)
        pa[nx] = total
        pb[nx] = total
    else:
        for copy in result(nx // STEP - 1):
            copy.start()
        for g in range(nx // STEP):
            for copy in result(g):
                copy.wait()


def close(k, diffusion, sums, hot, inn, kc, cap, mask, own, near, near0):
    last = k == ITERS - 1
    nx, rows, depth = cap.shape
    chans = inn.shape[1]
    n_pipes = 256
    args = [diffusion, *sums, hot, inn, kc, cap, mask, *own, *near]
    if k > 0:
        args += near0
    shape = lambda *dims: jax.ShapeDtypeStruct(dims, F32)
    scratch = [
        pltpu.VMEM((2, chans, nx * rows, 128), F32),
        pltpu.VMEM((2, 4, nx * rows, 128), F32),
        pltpu.VMEM((2, chans + 2, rows, depth), F32),
    ]
    if last:
        shapes = [shape(nx, rows, depth), shape(chans - 1, nx, rows, depth)]
        out_specs = [HB] * 2
        scratch += [
            pltpu.VMEM((nx, rows, depth), F32),
            pltpu.VMEM((chans - 1, nx, rows, depth), F32),
            pltpu.SemaphoreType.DMA((nx // STEP, 2)),
        ]
    else:
        shapes = [shape(2, nx, rows, 128), shape(2, chans, nx + 2, rows + 2 * TOP, 128)]
        shapes += [shape(chans, rows, depth)] * 2 + [shape(nx + 1, 8, n_pipes)] * 2
        out_specs = [VM] * 6
    return pl.pallas_call(
        functools.partial(close_kernel, k, last, nx, rows, chans),
        in_specs=[VM] * len(args),
        out_specs=out_specs,
        out_shape=shapes,
        scratch_shapes=scratch,
        compiler_params=pltpu.CompilerParams(vmem_limit_bytes=VLIM),
        cost_estimate=pl.CostEstimate(flops=2 * 10**7, bytes_accessed=10**7, transcendentals=0),
    )(*args)


def swap(x, axis, first_low):
    count = lax.axis_size(axis)
    pairs = []
    for low in range(first_low, count - 1, 2):
        pairs += [(low, low + 1), (low + 1, low)]
    return lax.ppermute(x, axis, pairs)


def beside_x(px1, px2):
    return [swap(px1, "gx", 0), swap(px2, "gx", 1)]


def beside_y(pa, pb, nx):
    count = lax.axis_size("gy")
    ya = swap(pa, "gy", 0)
    pair_sum = pa[nx:] + ya[nx:]
    pb = lax.dynamic_update_slice(pb, pair_sum, (nx, 0, 0))
    ring = []
    for low in range(1, count, 2):
        other = (low + 1) % count
        ring += [(low, other), (other, low)]
    yb = lax.ppermute(pb, "gy", ring)
    four = pair_sum + yb[nx:]
    far = lax.ppermute(four, "gy", [(i, (i + count // 2) % count) for i in range(count)])
    return [ya, yb], four + far


def body(
    adj_head,
    adj_species,
    cond,
    capacity,
    rate,
    diffusion,
    coupling,
    react,
    material,
    drain_mask,
    block_pipe,
    pipe_obs,
):
    nx = adj_head.shape[0]
    pipes = jnp.transpose(block_pipe, (0, 2, 1))
    *packs, pa, pb, hot = first(
        adj_head, adj_species, cond, capacity, drain_mask, pipes, pipe_obs
    )
    near_x = beside_x(*packs)
    near0 = None
    sums = []
    for k in range(ITERS):
        near_y, total = beside_y(pa, pb, nx)
        near = near_x + near_y
        near0 = near if k == 0 else near0
        sums.append(total)
        if k == 0:
            coef, kc, inn = first_inner(
                diffusion, coupling, react, rate, adj_head, material, capacity, adj_species, cond
            )
        else:
            inn = inner(diffusion, coupling, react, rate, h, coef, kc, st)
        own = [*packs, pa, pb]
        out = close(k, diffusion, sums, hot, inn, kc, capacity, drain_mask, own, near, near0)
        if k < ITERS - 1:
            h, st, *packs, pa, pb = out
            near_x = beside_x(*packs)
    return tuple(out)


def solution(mesh):
    return jax.shard_map(
        body,
        mesh=mesh,
        in_specs=(
            P("gx", "gy", None),
            P(None, "gx", "gy", None),
            P("gx", "gy", None),
            P("gx", "gy", None),
            P("gx", "gy", None),
            P(),
            P(),
            P(),
            P("gx", "gy", None),
            P("gx", "gy", None),
            P("gx", "gy", None),
            P(None, "gx", "gy"),
        ),
        out_specs=(P("gx", "gy", None), P(None, "gx", "gy", None)),
        check_vma=False,
    )
```

```python
import functools

import jax
import jax.numpy as jnp
from jax import lax
from jax.experimental import pallas as pl
from jax.experimental.pallas import tpu as pltpu
from jax.sharding import PartitionSpec as P

ITERS = 3
time_step = 0.08
drain_gain = 0.5

F32 = jnp.float32
BF16 = jnp.bfloat16
HB = pl.BlockSpec(memory_space=pltpu.HBM)
ANY = pl.BlockSpec(memory_space=pl.ANY)
VM = pl.BlockSpec(memory_space=pltpu.VMEM)
SM = pl.BlockSpec(memory_space=pltpu.SMEM)
TOP = 8
STEP = 4
INNER_STEP = 8
RB = 16


VLIM = 14 * 2**20
LANES = (slice(0, 128), slice(128, 256))


def split(x, pieces):
    out = []
    for _ in range(pieces):
        piece = x.astype(BF16)
        out.append(piece)
        x = x - piece.astype(F32)
    return out


def block_onehots(bp, hot):
    nx, blocks, rows = bp.shape
    n_pipes = hot.shape[2]
    flat = bp[...].astype(F32).reshape(nx * blocks, rows)
    flat = jnp.concatenate([flat, jnp.zeros((128 - nx * blocks, rows), F32)], axis=0)
    tall = jnp.transpose(jnp.concatenate([flat, jnp.zeros((128, 128 - rows), F32)], axis=1))
    pipe = lax.broadcasted_iota(jnp.int32, (rows, n_pipes), 1).astype(F32)
    for x in range(nx):
        for j in range(blocks):
            n = x * blocks + j
            match = tall[:rows, n : n + 1] == pipe
            hot[j, x * rows : (x + 1) * rows, :] = match.astype(BF16)


def turn(x, by):
    return pltpu.roll(x, (-by) % 128, 1)


def halve(values):
    low = lax.broadcasted_iota(jnp.int32, values[0].shape, 1) < 64
    return [
        jnp.where(low, a, b) + turn(jnp.where(low, b, a), 64)
        for a, b in zip(values[::2], values[1::2])
    ]


def merge(level):
    lane = lax.broadcasted_iota(jnp.int32, level[0].shape, 1)
    for width in (32, 16):
        low = lane & width == 0
        level = [
            jnp.where(low, a, b) + jnp.where(low, turn(a, width), turn(b, -width))
            for a, b in zip(level[::2], level[1::2])
        ]
    return level[0]


SUM_LANE = [64 * (c & 1) + 32 * (c >> 1 & 1) + 16 * (c >> 2 & 1) for c in range(8)]
CHUNK = 128


def block_sums(half, j):
    lane = lax.broadcasted_iota(jnp.int32, (16, 128), 1) // 16
    chan = lax.broadcasted_iota(jnp.int32, (16, 128), 0)
    group = 4 * (chan & 1) + 2 * (chan >> 1 & 1) + (chan >> 2 & 1)
    pick = ((lane == group) & (chan < 8)).astype(BF16)
    out = []
    for r in range(0, half.shape[2], CHUNK):
        merged = merge([half[j, c, r : r + CHUNK, :] for c in range(4)])
        total = None
        for piece in split(merged, 3)[::-1]:
            part = lax.dot_general(
                pick, piece, (((1,), (1,)), ((), ())), preferred_element_type=F32
            )
            total = part if total is None else total + part
        out.append(total)
    return jnp.concatenate(out, axis=1)[:8]


def pipe_sums(half, hot):
    total = None
    for j in range(2):
        rows = block_sums(half, j)
        stack = jnp.concatenate(split(rows, 3) + [jnp.zeros(rows.shape, BF16)], axis=0)
        part = jnp.dot(stack, hot[j], preferred_element_type=F32)
        total = part if total is None else total + part
    return (total[16:24] + total[8:16]) + total[:8]


def edge_flags():
    gx, gy = lax.axis_index("gx"), lax.axis_index("gy")
    return gx % 2 == 0, gy % 2 == 0, gy


def clear_rim(ref, nx, rows, *lead):
    tile = jnp.zeros((TOP, 128), F32)
    for j in range(2):
        for x in (0, nx + 1):
            for r in range(0, rows + 2 * TOP, TOP):
                ref[(j, *lead, x, slice(r, r + TOP))] = tile


def first_kernel(
    nx, rows, chans, h, sp, cond, cap, mask, bp, obs, px1, px2, pa, pb, hot,
    half, vh, vs, vk, vcap, vmask, sem, tiny_sem, vbp, vobs
):
    even_x, even_y, gy = edge_flags()
    n_pipes = pa.shape[2]

    def chunk(g):
        at = pl.ds(g * STEP, STEP)
        pairs = [(sp.at[:, at], vs.at[:, at])]
        for src, dst in ((h, vh), (cond, vk), (cap, vcap), (mask, vmask)):
            pairs.append((src.at[at], dst.at[at]))
        return [pltpu.make_async_copy(a, b, sem.at[g, n]) for n, (a, b) in enumerate(pairs)]

    tiny = [pltpu.make_async_copy(bp, vbp, tiny_sem.at[0]), pltpu.make_async_copy(obs, vobs, tiny_sem.at[1])]
    for copy in tiny:
        copy.start()
    for g in range(nx // STEP):
        for copy in chunk(g):
            copy.start()
    for copy in tiny:
        copy.wait()
    block_onehots(vbp, hot)

    def planes(i, carry):
        @pl.when(i % (STEP // 2) == 0)
        def _():
            for copy in chunk(i // (STEP // 2)):
                copy.wait()

        work(2 * i)
        work(2 * i + 1)
        return carry

    def work(x):
        for j, part in enumerate(LANES):
            cd = vk[x, :, part]
            head = vh[x, :, part]
            m = vmask[x, :, part].astype(F32)
            scaled = time_step * head / vcap[x, :, part]
            species = [vs[c, x, :, part] for c in range(chans - 1)]
            for c, field in enumerate([scaled, *species, cd]):
                lo, hi = field[0:1], field[rows - 1 : rows]
                pa[x, c : c + 1, part] = jnp.where(even_y, hi, lo)
                pb[x, c : c + 1, part] = jnp.where(even_y, lo, hi)
            sums = halve([cd * m * head] + [v * m for v in species] + [m])
            place = pl.ds(x * rows, rows)
            for c in range(4):
                half[j, c, place, :] = sums[c]

    lax.fori_loop(0, nx // 2, planes, 0)

    def send(dst, x):
        dst[0] = time_step * vh[x] / vcap[x]
        for c in range(chans - 1):
            dst[c + 1] = vs[c, x]
        dst[chans] = vk[x]

    @pl.when(even_x)
    def _():
        send(px1, nx - 1)
        send(px2, 0)

    @pl.when(jnp.logical_not(even_x))
    def _():
        send(px1, 0)
        send(px2, nx - 1)

    total = pipe_sums(half, hot)
    small = vobs[:, 0, :]
    wide = jnp.concatenate([small] * (n_pipes // small.shape[1]), axis=1)
    place = lax.broadcasted_iota(jnp.int32, wide.shape, 1) // small.shape[1]
    mine = jnp.where(place == gy, wide, 0.0)
    second = jnp.concatenate([mine, jnp.zeros((1, n_pipes), F32)], axis=0)
    for dst in (pa, pb):
        dst[nx] = total
        dst[nx + 1] = second


def first(h, sp, cond, cap, mask, bp, obs):
    nx, rows, depth = h.shape
    chans = sp.shape[0] + 1
    n_pipes = 256
    shape = lambda *dims: jax.ShapeDtypeStruct(dims, F32)
    field = lambda dtype: pltpu.VMEM((nx, rows, depth), dtype)
    return pl.pallas_call(
        functools.partial(first_kernel, nx, rows, chans),
        in_specs=[HB] * 7,
        out_specs=[VM] * 5,
        out_shape=[
            shape(chans + 1, rows, depth),
            shape(chans + 1, rows, depth),
            shape(nx + 2, 8, n_pipes),
            shape(nx + 2, 8, n_pipes),
            jax.ShapeDtypeStruct((2, nx * rows, n_pipes), BF16),
        ],
        scratch_shapes=[
            pltpu.VMEM((2, 4, nx * rows, 128), F32),
            field(F32),
            pltpu.VMEM(sp.shape, F32),
            field(F32),
            field(F32),
            field(jnp.int32),
            pltpu.SemaphoreType.DMA((nx // STEP, 5)),
            pltpu.SemaphoreType.DMA((2,)),
            pltpu.VMEM(bp.shape, jnp.int32),
            pltpu.VMEM(obs.shape, F32),
        ],
        compiler_params=pltpu.CompilerParams(vmem_limit_bytes=53 * 2**20),
        cost_estimate=pl.CostEstimate(flops=10**7, bytes_accessed=8 * 10**6, transcendentals=0),
    )(h, sp, cond, cap, mask, bp, obs)


def inner_kernel(fresh, nx, rows, chans, diffusion, coupling, *refs):
    if fresh:
        react, rate, h, mat, cap, sp, cond, coef, kc, out, st, vh, vcap, sem = refs
    else:
        rate, h, coef, kc, st, out = refs
    nsp = chans - 1
    both = range(2)
    gains = diffusion[...].reshape(1, nsp)
    heads = coupling[...].reshape(1, nsp)
    diffusion = [jnp.broadcast_to(gains[:, c : c + 1], (RB, 128)) for c in range(nsp)]
    coupling = [jnp.broadcast_to(heads[:, c : c + 1], (RB, 128)) for c in range(nsp)]
    lane = lax.broadcasted_iota(jnp.int32, (RB, 128), 1)
    first_lane, last_lane = lane == 0, lane == 127

    def updown(pair):
        left = [turn(v, -1) for v in pair]
        right = [turn(v, 1) for v in pair]
        up = [jnp.where(first_lane, 0.0, left[0]), jnp.where(first_lane, left[0], left[1])]
        down = [jnp.where(last_lane, right[1], right[0]), jnp.where(last_lane, 0.0, right[1])]
        return up, down

    def chunk(g):
        at, into = pl.ds(g * INNER_STEP, INNER_STEP), pl.ds(g * INNER_STEP + 1, INNER_STEP)
        inside = pl.ds(TOP, rows)
        pairs = []
        for j, part in enumerate((pl.ds(0, 128), pl.ds(128, 128))):
            pairs.append((sp.at[:, at, :, part], st.at[j, pl.ds(1, nsp), into, inside, :]))
            pairs.append((cond.at[at, :, part], kc.at[j, into, inside, :]))
        for src, dst in ((h, vh), (cap, vcap)):
            pairs.append((src.at[at], dst.at[at]))
        return [pltpu.make_async_copy(a, b, sem.at[g, n]) for n, (a, b) in enumerate(pairs)]

    def arrive(g):
        for copy in chunk(g):
            copy.wait()

    def scale(x):
        for j in both:
            scaled = time_step * vh[x, :, LANES[j]] / vcap[x, :, LANES[j]]
            st[j, 0, x + 1, TOP : TOP + rows, :] = scaled

    if fresh:
        for g in range(nx // INNER_STEP):
            for copy in chunk(g):
                copy.start()
        for c in range(chans):
            clear_rim(st, nx, rows, c)
        clear_rim(kc, nx, rows)

        def rims(x, carry):
            rim = jnp.zeros((1, 128), F32)
            for j in both:
                for at in (slice(TOP - 1, TOP), slice(TOP + rows, TOP + rows + 1)):
                    for c in range(chans):
                        st[j, c, x, at, :] = rim
                    kc[j, x, at, :] = rim
            return carry

        lax.fori_loop(1, nx + 1, rims, 0)
        arrive(0)
        scale(0)
        scale(1)
        scale(2)

    def planes(i, carry):
        x = 2 * i
        if fresh:

            @pl.when((x % INNER_STEP == 0) & (x < nx - INNER_STEP))
            def _():
                arrive(x // INNER_STEP + 1)

        plane(x)
        plane(x + 1)
        if fresh:
            scale(jnp.minimum(x + 3, nx - 1))
            scale(jnp.minimum(x + 4, nx - 1))
        return carry

    def plane(x):
        for r in range(0, rows, RB):
            at = TOP + r
            body = slice(r, r + RB)

            def sides(ref, *lead):
                near = [
                    [
                        ref[(j, *lead, x, slice(at, at + RB))],
                        ref[(j, *lead, x + 2, slice(at, at + RB))],
                        ref[(j, *lead, x + 1, slice(at - 1, at - 1 + RB))],
                        ref[(j, *lead, x + 1, slice(at + 1, at + 1 + RB))],
                    ]
                    for j in both
                ]
                return [ref[(j, *lead, x + 1, slice(at, at + RB))] for j in both], near

            rt = [time_step * rate[x, body, LANES[j]] for j in both]
            if fresh:
                mt = [mat[x, body, LANES[j]] for j in both]
                odd = [v % 2 == 1 for v in mt]
                high = [v >= 2 for v in mt]

            c_mid, c_near = sides(kc)
            s_mid, s_near = sides(st, 0)
            c_up, c_down = updown(c_mid)
            s_up, s_down = updown(s_mid)
            flow = []
            for j in both:
                acc = None
                near_c = c_near[j] + [c_up[j], c_down[j]]
                near_s = s_near[j] + [s_up[j], s_down[j]]
                for oc, os in zip(near_c, near_s):
                    term = (c_mid[j] + oc) * (os - s_mid[j])
                    acc = term if acc is None else acc + term
                flow.append(0.5 * acc)
            mids = []
            outs = [[None] * chans for _ in both]
            for c in range(nsp):
                mid, near = sides(st, c + 1)
                up, down = updown(mid)
                kd = time_step * diffusion[c]
                mids.append(mid)
                for j in both:
                    n4 = (near[j][0] + near[j][1]) + (near[j][2] + near[j][3])
                    n6 = n4 + (up[j] + down[j])
                    outs[j][c + 1] = mid[j] + kd * (n6 - 6.0 * mid[j])
            for j in both:
                source = None
                for c in range(nsp):
                    term = coupling[c] * mids[c][j]
                    source = term if source is None else source + term
                head = vh[x, body, LANES[j]] if fresh else h[j, x, body]
                out[j, 0, x, body, :] = head + flow[j] + rt[j] * source
            for s in range(nsp):
                acc = [outs[j][s + 1] for j in both]
                for t in range(nsp):
                    n = s * nsp + t
                    for j in both:
                        if fresh:
                            r0, r1, r2, r3 = (react[i, t, s] for i in range(4))
                            w = jnp.where(
                                high[j], jnp.where(odd[j], r3, r2), jnp.where(odd[j], r1, r0)
                            )
                            w = w * -rt[j]
                            coef[j, n, x, body, :] = w
                        else:
                            w = coef[j, n, x, body, :]
                        acc[j] = acc[j] + w * mids[t][j]
                for j in both:
                    out[j, s + 1, x, body, :] = acc[j]

    lax.fori_loop(0, nx // 2, planes, 0)


def inner(diffusion, coupling, react, rate, h, coef, kc, st):
    nx, rows, _ = rate.shape
    chans = st.shape[1]
    return pl.pallas_call(
        functools.partial(inner_kernel, False, nx, rows, chans),
        in_specs=[VM] * 2 + [VM] * 5,
        out_specs=VM,
        out_shape=jax.ShapeDtypeStruct((2, chans, nx, rows, 128), F32),
        compiler_params=pltpu.CompilerParams(vmem_limit_bytes=2 * 2**20),
        cost_estimate=pl.CostEstimate(flops=6 * 10**7, bytes_accessed=3 * 10**7, transcendentals=0),
    )(diffusion, coupling, rate, h, coef, kc, st)


def first_inner(diffusion, coupling, react, rate, h, mat, cap, sp, cond):
    nx, rows, depth = rate.shape
    nsp = sp.shape[0]
    chans = nsp + 1
    shape = lambda *dims: jax.ShapeDtypeStruct(dims, F32)
    padded = (nx + 2, rows + 2 * TOP, 128)
    return pl.pallas_call(
        functools.partial(inner_kernel, True, nx, rows, chans),
        in_specs=[VM, VM, SM, VM, HB, VM, HB, HB, HB],
        out_specs=[VM] * 3,
        out_shape=[
            shape(2, nsp * nsp, nx, rows, 128),
            shape(2, *padded),
            shape(2, chans, nx, rows, 128),
        ],
        scratch_shapes=[
            pltpu.VMEM((2, chans, *padded), F32),
            pltpu.VMEM((nx, rows, depth), F32),
            pltpu.VMEM((nx, rows, depth), F32),
            pltpu.SemaphoreType.DMA((nx // INNER_STEP, 6)),
        ],
        compiler_params=pltpu.CompilerParams(vmem_limit_bytes=12 * 2**20),
        cost_estimate=pl.CostEstimate(flops=6 * 10**7, bytes_accessed=3 * 10**7, transcendentals=0),
    )(diffusion, coupling, react, rate, h, mat, cap, sp, cond)


def close_kernel(k, last, nx, rows, chans, *refs):
    refs = list(refs)
    take = lambda n: [refs.pop(0) for _ in range(n)]
    (diffusion,) = take(1)
    sums = take(k + 1)
    hot, inn, kc, cap, mask = take(5)
    ox1, ox2, oya, oyb = take(4)
    xr1, xr2, ya, yb = take(4)
    cx1, cx2, cya, cyb = (xr1, xr2, ya, yb) if k == 0 else take(4)
    if last:
        oh, osp = take(2)
    else:
        oh, ost, px1, px2, pa, pb = take(6)
    ansb, half, xh = take(3)
    if last:
        th, tsp, sem = take(3)

    n_pipes = 256
    nsp = chans - 1
    even_x, even_y, gy = edge_flags()
    last_y = lax.axis_size("gy") - 1

    t0 = sums[0]
    root = jnp.sqrt(t0[0, 7:8, :] + 1.0)
    observed = t0[1]
    row = lax.broadcasted_iota(jnp.int32, (8, n_pipes), 0)
    answer = jnp.tanh(observed - t0[0] / root)
    if k > 0:
        weight = drain_gain * jnp.where(row == 0, sums[1][0, 7:8, :], t0[0, 7:8, :])
    for later in sums[1:]:
        answer = jnp.tanh(observed - (later[0] + answer * weight) / root)
    answer = drain_gain * answer
    tall = jnp.transpose(jnp.concatenate([answer, jnp.zeros((120, n_pipes), F32)], axis=0))
    pieces = jnp.concatenate(split(tall, 2), axis=1)
    part_of = lax.broadcasted_iota(jnp.int32, (256, 256), 1) // 128
    chan_of = lax.broadcasted_iota(jnp.int32, (256, 256), 0) % 128
    for j in range(2):
        picked = jnp.dot(hot[j], pieces, preferred_element_type=F32).astype(BF16)
        for c in range(0, chans, 2):
            spread = (part_of + c == chan_of).astype(BF16)
            wide = jnp.dot(picked, spread, preferred_element_type=F32)
            ansb[j, c] = wide[:, :128]
            if c + 1 < chans:
                ansb[j, c + 1] = wide[:, 128:]

    a_lo = jnp.where(even_y, 0.0, 1.0)
    b_lo = jnp.where(even_y & (gy > 0), 1.0, 0.0)
    a_hi = jnp.where(even_y, 1.0, 0.0)
    b_hi = jnp.where(even_y | (gy == last_y), 0.0, 1.0)
    row = lax.broadcasted_iota(jnp.int32, (8, 128), 0)
    top, bottom = row == 0, row == 7
    gains = jnp.zeros((8, 128), F32)
    share = time_step * diffusion[...].reshape(1, nsp)
    shares = [share[:, c : c + 1] for c in range(nsp)]
    for c in range(nsp):
        gains = jnp.where(row == c + 1, shares[c], gains)
    rim = jnp.zeros((TOP, 128), F32)
    if not last:
        for c in range(chans):
            clear_rim(ost, nx, rows, c)

    def pull(c_mid, s_mid, c_far, s_far):
        return 0.5 * ((c_mid + c_far) * s_far - c_far * s_mid)

    def keep(n, near, cnear, own):
        xh[n, chans + 1] = own[0]
        for c in range(chans):
            xh[n, c] = near[c]
        xh[n, chans] = cnear[chans]

    @pl.when(even_x)
    def _():
        keep(0, xr2, cx2, ox2)
        keep(1, xr1, cx1, ox1)

    @pl.when(jnp.logical_not(even_x))
    def _():
        keep(0, xr1, cx1, ox1)
        keep(1, xr2, cx2, ox2)

    def work(x, rim_at):
        for j, part in enumerate(LANES):
            def rims_of(ra, rb, wa, wb):
                return ra[x, :, part] * wa + rb[x, :, part] * wb

            m = mask[x, :, part].astype(F32)
            c_all = kc[j, x + 1, TOP : TOP + rows, :]
            add = []
            for at, wa, wb in ((0, a_lo, b_lo), (rows - 1, a_hi, b_hi)):
                far = rims_of(ya, yb, wa, wb)
                c_far = far if k == 0 else rims_of(cya, cyb, wa, wb)
                c_far = c_far[chans : chans + 1]
                s_mid = jnp.where(even_y == (at > 0), oya[x, 0:1, part], oyb[x, 0:1, part])
                head = pull(kc[j, x + 1, TOP + at : TOP + at + 1, :], s_mid, c_far, far[0:1])
                add.append((head, gains * far))
            values = []
            for c in range(chans):
                v = inn[j, c, x]
                lo, hi = ((a[0] if c == 0 else a[1][c : c + 1]) for a in add)
                v = jnp.concatenate(
                    [
                        v[:8] + jnp.where(top, lo, 0.0),
                        v[8 : rows - 8],
                        v[rows - 8 :] + jnp.where(bottom, hi, 0.0),
                    ],
                    axis=0,
                )
                if rim_at is not None:
                    far = xh[rim_at, c, :, part]
                    if c == 0:
                        v = v + pull(c_all, xh[rim_at, chans + 1, :, part], xh[rim_at, chans, :, part], far)
                    else:
                        v = v + shares[c - 1] * far
                values.append(v)
            if not last:
                drained = [v * m for v in values]
                drained[0] = drained[0] * c_all
                drained.append(c_all * m)
                for c, v in enumerate(halve(drained)):
                    half[j, c, pl.ds(x * rows, rows), :] = v
            for c, v in enumerate(values):
                v = v + m * ansb[j, c, pl.ds(x * rows, rows), :]
                if last:
                    if c == 0:
                        th[x, :, part] = v
                    else:
                        tsp[c - 1, x, :, part] = v
                    continue
                if c == 0:
                    oh[j, x] = v
                    v = time_step * v / cap[x, :, part]
                ost[j, c, x + 1, TOP : TOP + rows, :] = v
                ost[j, c, x + 1, 0:TOP, :] = rim
                ost[j, c, x + 1, TOP + rows : 2 * TOP + rows, :] = rim
                lo, hi = v[0:1], v[rows - 1 : rows]
                pa[x, c : c + 1, part] = jnp.where(even_y, hi, lo)
                pb[x, c : c + 1, part] = jnp.where(even_y, lo, hi)

    def result(g):
        at = pl.ds(g * STEP, STEP)
        pairs = [(th.at[at], oh.at[at]), (tsp.at[:, at], osp.at[:, at])]
        return [pltpu.make_async_copy(a, b, sem.at[g, n]) for n, (a, b) in enumerate(pairs)]

    def planes(i, carry):
        x = 2 * i
        work(x - 1, None)
        if last:

            @pl.when(x % STEP == 0)
            def _():
                for copy in result(x // STEP - 1):
                    copy.start()

        work(x, None)
        return carry

    work(0, 0)
    work(nx - 1, 1)
    lax.fori_loop(1, nx // 2, planes, 0)
    if not last:

        def send(dst, x):
            for c in range(chans):
                for j, part in enumerate(LANES):
                    dst[c, :, part] = ost[j, c, x + 1, TOP : TOP + rows, :]

        @pl.when(even_x)
        def _():
            send(px1, nx - 1)
            send(px2, 0)

        @pl.when(jnp.logical_not(even_x))
        def _():
            send(px1, 0)
            send(px2, nx - 1)

        total = pipe_sums(half, hot)
        pa[nx] = total
        pb[nx] = total
    else:
        for copy in result(nx // STEP - 1):
            copy.start()
        for g in range(nx // STEP):
            for copy in result(g):
                copy.wait()


def close(k, diffusion, sums, hot, inn, kc, cap, mask, own, near, near0):
    last = k == ITERS - 1
    nx, rows, depth = cap.shape
    chans = inn.shape[1]
    n_pipes = 256
    args = [diffusion, *sums, hot, inn, kc, cap, mask, *own, *near]
    if k > 0:
        args += near0
    shape = lambda *dims: jax.ShapeDtypeStruct(dims, F32)
    scratch = [
        pltpu.VMEM((2, chans, nx * rows, 128), F32),
        pltpu.VMEM((2, 4, nx * rows, 128), F32),
        pltpu.VMEM((2, chans + 2, rows, depth), F32),
    ]
    if last:
        shapes = [shape(nx, rows, depth), shape(chans - 1, nx, rows, depth)]
        out_specs = [HB] * 2
        scratch += [
            pltpu.VMEM((nx, rows, depth), F32),
            pltpu.VMEM((chans - 1, nx, rows, depth), F32),
            pltpu.SemaphoreType.DMA((nx // STEP, 2)),
        ]
    else:
        shapes = [shape(2, nx, rows, 128), shape(2, chans, nx + 2, rows + 2 * TOP, 128)]
        shapes += [shape(chans, rows, depth)] * 2 + [shape(nx + 1, 8, n_pipes)] * 2
        out_specs = [VM] * 6
    return pl.pallas_call(
        functools.partial(close_kernel, k, last, nx, rows, chans),
        in_specs=[VM] * len(args),
        out_specs=out_specs,
        out_shape=shapes,
        scratch_shapes=scratch,
        compiler_params=pltpu.CompilerParams(vmem_limit_bytes=VLIM),
        cost_estimate=pl.CostEstimate(flops=2 * 10**7, bytes_accessed=10**7, transcendentals=0),
    )(*args)


def swap(x, axis, first_low):
    count = lax.axis_size(axis)
    pairs = []
    for low in range(first_low, count - 1, 2):
        pairs += [(low, low + 1), (low + 1, low)]
    return lax.ppermute(x, axis, pairs)


def beside_x(px1, px2):
    return [swap(px1, "gx", 0), swap(px2, "gx", 1)]


def beside_y(pa, pb, nx):
    count = lax.axis_size("gy")
    ya = swap(pa, "gy", 0)
    pair_sum = pa[nx:] + ya[nx:]
    pb = lax.dynamic_update_slice(pb, pair_sum, (nx, 0, 0))
    ring = []
    for low in range(1, count, 2):
        other = (low + 1) % count
        ring += [(low, other), (other, low)]
    yb = lax.ppermute(pb, "gy", ring)
    four = pair_sum + yb[nx:]
    far = lax.ppermute(four, "gy", [(i, (i + count // 2) % count) for i in range(count)])
    return [ya, yb], four + far


def body(
    adj_head,
    adj_species,
    cond,
    capacity,
    rate,
    diffusion,
    coupling,
    react,
    material,
    drain_mask,
    block_pipe,
    pipe_obs,
):
    nx = adj_head.shape[0]
    pipes = jnp.transpose(block_pipe, (0, 2, 1))
    *packs, pa, pb, hot = first(
        adj_head, adj_species, cond, capacity, drain_mask, pipes, pipe_obs
    )
    near_x = beside_x(*packs)
    near0 = None
    sums = []
    for k in range(ITERS):
        near_y, total = beside_y(pa, pb, nx)
        near = near_x + near_y
        near0 = near if k == 0 else near0
        sums.append(total)
        if k == 0:
            coef, kc, inn = first_inner(
                diffusion, coupling, react, rate, adj_head, material, capacity, adj_species, cond
            )
        else:
            inn = inner(diffusion, coupling, react, rate, h, coef, kc, st)
        own = [*packs, pa, pb]
        out = close(k, diffusion, sums, hot, inn, kc, capacity, drain_mask, own, near, near0)
        if k < ITERS - 1:
            h, st, *packs, pa, pb = out
            near_x = beside_x(*packs)
    return tuple(out)


def solution(mesh):
    return jax.shard_map(
        body,
        mesh=mesh,
        in_specs=(
            P("gx", "gy", None),
            P(None, "gx", "gy", None),
            P("gx", "gy", None),
            P("gx", "gy", None),
            P("gx", "gy", None),
            P(),
            P(),
            P(),
            P("gx", "gy", None),
            P("gx", "gy", None),
            P("gx", "gy", None),
            P(None, "gx", "gy"),
        ),
        out_specs=(P("gx", "gy", None), P(None, "gx", "gy", None)),
        check_vma=False,
    )
```
